128 devices in a mesh: bx: 16 (over y_lo, z, core), by: 8 (over x, y_hi).
Axes of the slice: x: 4, y: 4 (y_hi: 2, y_lo: 2; y = y_hi * 2 + y_lo), z: 4, core: 2. Of those that a mesh axis runs over, the one named last changes fastest.
Arguments:
- charges: bfloat16 [262144, 128], P(('bx', 'by')), may hold values from -6 to 6
- weight_tiles: bfloat16 [32, 128, 512], replicated, may hold values from 0 to 0.14941406
- block_shape: int32 [262144], P(('bx', 'by')), may hold values from 0 to 31
- block_box: int32 [262144], P(('bx', 'by')), may hold values from 0 to 32767
- live_blocks: int32 [128], P(('bx', 'by')), may hold values from 1 to 2048, 131072 in all
Outputs:
- coarse: float32 [128, 2048, 512], P('bx', 'by')
The draws below stay inside these ranges and needn't reach their ends.
Inputs may be any that keep to these rules, and one draw needn't show every extreme that they name: `live_blocks`: live slots of a device are its first ones; some device uses all 2048 slots.
All inputs are finite; a program needn't handle non-finite values.
Results may differ from the reference program's by a relative error of at most 0.0003.
Values may be sent and summed in bfloat16 or wider, within the bound.
No kernel may reach another device: no remote copies, remote signals or barrier semaphores. Data moves between devices by JAX's collectives and lax.ppermute only.
A program may use at most 192 MiB of HBM per device.

```python
import math
import jax
import jax.numpy as jnp
import numpy as np
from jax import lax

CX = 64
CY = 256
NZ = 128
ATOMS = 128
CELLS = 512
SHAPES = 32
BLK_DEV = 2048
NX = 1024
NY = 2048
BLOCKS = 262144
BOXES_DEV = 32768
N_BX = 16
N_BY = 8


def touch_ends(array, rng, low, top_value):
    longest = array.shape.index(max(array.shape))
    spots = []
    for shift in (0, 1):
        where = [jax.random.randint(jax.random.fold_in(rng, axis), (), 0, length) for axis, length in enumerate(array.shape)]
        where[longest] = (where[longest] + shift) % array.shape[longest]
        spots.append(tuple(where))
    return array.at[spots[0]].set(low).at[spots[1]].set(top_value)


def block_levels(stream_key, extent, pieces, low, largest):
    gain = 1.0
    for axis_at, parts in pieces:
        draws = jax.random.uniform(jax.random.fold_in(jax.random.fold_in(stream_key, 6), axis_at), (parts,), jnp.float32, low / len(pieces), largest / len(pieces))
        gain = gain * jnp.repeat(jnp.exp(draws), extent[axis_at] // parts).reshape((-1,) + (1,) * (len(extent) - 1 - axis_at))
    return gain


def profile(number_of, total, limit, slope):
    weights = [(1 << 20) // math.isqrt(standing ** slope) + 1 for standing in range(2, number_of + 1)]
    spare, counts = total - limit - (number_of - 1), [1] * (number_of - 1)
    while spare > 0:
        candidates = [i for i in range(number_of - 1) if counts[i] < limit]
        pool, remaining = sum([weights[i] for i in candidates]), spare
        for i in candidates:
            more = min(limit - counts[i], max(1, remaining * weights[i] // pool), spare)
            counts[i] = counts[i] + more
            spare = spare - more
    return np.array([limit] + counts)


def uneven_parts(key, number_of, total, limit, skew):
    if number_of == 2:
        one = jax.random.randint(key, (), max(1, total - limit), min(limit, total - 1) + 1)
        return jnp.stack([one, total - one])
    sizes = jnp.asarray(profile(number_of, total, limit, skew), jnp.int32)
    couples = (number_of - 1) // 2
    giver, taker = sizes[1:1 + 2 * couples:2], sizes[2:2 + 2 * couples:2]
    room = jnp.minimum(giver - 1, limit - taker)
    passed = jax.random.randint(jax.random.fold_in(key, 1), (couples,), 0, 1 << 20) % (room + 1)
    sizes = sizes.at[1:1 + 2 * couples:2].set(giver - passed).at[2:2 + 2 * couples:2].set(taker + passed)
    return sizes[jax.random.permutation(jax.random.fold_in(key, 2), number_of)]


def normal_values(rng, dims, spread, most, shards=(), kind=jnp.bfloat16):
    drawn = spread * jax.random.normal(rng, dims, jnp.float32)
    if shards:
        drawn = drawn * block_levels(rng, dims, shards, -0.22, 0.18)
    return jnp.clip(drawn, -most, most).astype(kind)


def setup_inputs(seed: int = 0) -> dict:
    arg_keys = jax.random.split(jax.random.key(seed), 6)
    charges = normal_values(arg_keys[0], (BLOCKS, ATOMS), 1.0, 6.0, ((0, 128),))
    weight_tiles = jnp.clip(jax.random.uniform(arg_keys[1], (SHAPES, ATOMS, CELLS), jnp.float32, 0.0, 0.14941406), 0.0, 0.14941406).astype(jnp.bfloat16)
    block_shape = touch_ends(jax.random.randint(arg_keys[2], (BLOCKS,), 0, SHAPES), jax.random.fold_in(arg_keys[2], 1), 0, SHAPES - 1).astype(jnp.int32)
    block_box = touch_ends(jax.random.randint(arg_keys[3], (BLOCKS,), 0, BOXES_DEV), jax.random.fold_in(arg_keys[3], 1), 0, BOXES_DEV - 1).astype(jnp.int32)
    live_blocks = uneven_parts(arg_keys[4], N_BX * N_BY, N_BX * N_BY * BLK_DEV // 2, BLK_DEV, 2).astype(jnp.int32)
    return dict(charges=charges, weight_tiles=weight_tiles, block_shape=block_shape, block_box=block_box, live_blocks=live_blocks)


def restrict(field):
    return (6.0 * field + 4.0 * (jnp.roll(field, -1, axis=2) + jnp.roll(field, 1, axis=2)) + jnp.roll(field, -2, axis=2) + jnp.roll(field, 2, axis=2)) / 8.0


def reference(charges, weight_tiles, block_shape, block_box, live_blocks):
    devices = N_BX * N_BY
    group = min(256, BLK_DEV // 2)
    per_q = charges.reshape(devices, BLK_DEV // group, group, ATOMS)
    per_s = block_shape.reshape(devices, BLK_DEV // group, group)
    per_b = block_box.reshape(devices, BLK_DEV)
    cell = jnp.arange(CELLS, dtype=jnp.int32)
    off_x = cell // 64
    off_y = (cell // 8) % 8
    off_z = cell % 8
    ybox = CY // 4
    zbox = NZ // 4

    def one_group(items):
        qg, sg = items
        table = weight_tiles[sg].astype(jnp.float32)
        return jnp.einsum("ba,bac->bc", qg.astype(jnp.float32), table)

    def per_device(grid, items):
        dev, qd, sd, bd, live = items
        slot = jnp.arange(BLK_DEV, dtype=jnp.int32).reshape(BLK_DEV // group, group)
        qd = jnp.where((slot < live)[:, :, None], qd, jnp.zeros_like(qd))
        tiles = lax.map(one_group, (qd, sd)).reshape(BLK_DEV, CELLS)
        row = dev // N_BY
        col = dev % N_BY
        ux = bd // (ybox * zbox)
        vy = (bd // zbox) % ybox
        wz = bd % zbox
        gx = (row * CX + 4 * ux[:, None] - 2 + off_x[None, :]) % NX
        gy = (col * CY + 4 * vy[:, None] - 2 + off_y[None, :]) % NY
        gz = (4 * wz[:, None] - 2 + off_z[None, :]) % NZ
        flat = ((gx * NY + gy) * NZ + gz).reshape(-1)
        grid = grid.at[flat].add(tiles.reshape(-1))
        return grid, None

    start = jnp.zeros((NX * NY * NZ,), jnp.float32)
    grid, _ = lax.scan(per_device, start, (jnp.arange(devices, dtype=jnp.int32), per_q, per_s, per_b, live_blocks))
    field = grid.reshape(NX, NY, NZ).transpose(2, 1, 0)
    return restrict(field)[:, :, ::2]
```

```python
import jax
import jax.numpy as jnp
import numpy as np
from jax import lax
from jax.experimental import pallas as pl
from jax.experimental.pallas import tpu as pltpu
from jax.sharding import PartitionSpec as P

NZ = 128
GROUP = 256
BATCH = 16
KZ = 16
UROWS = 18
VSLOTS = 36
PLANE = UROWS * VSLOTS
GROWS = 4 * KZ * PLANE
SPARE = 256
VOUT = 34
TAIL = VOUT * 16
SENT = TAIL + 80
WIRE = jnp.int16
LEVELS = 32700.0
SCALE_ROW = TAIL + 34


def restriction():
    coef = [1.0, 4.0, 6.0, 4.0, 1.0]
    table = np.zeros((512, 384), np.float32)
    for p in range(8):
        for mm in range(6):
            tap = p + 4 - 2 * mm
            if not 0 <= tap < 5:
                continue
            for q in range(8):
                for r in range(8):
                    lane = (mm % 2) * 64 + ((r - 2) % 8) * 8 + (q - 2) % 8
                    table[(p * 8 + q) * 8 + r, (mm // 2) * 128 + lane] = coef[tap] / 8.0
    return table


def spread_kernel(base_ref, clash_ref, live_ref, q_ref, s_ref, w_ref, r_ref, out_ref, grid_ref, pick_ref, tile_ref, plane_ref):
    k = pl.program_id(0)
    shapes_n = w_ref.shape[0] // 128

    @pl.when(k == 0)
    def _():
        def clear(step, carry):
            grid_ref[pl.ds(pl.multiple_of(step * 256, 256), 256), :] = jnp.zeros((256, 128), jnp.float32)
            return carry

        lax.fori_loop(0, (GROWS + SPARE) // 256, clear, 0)

        def one_group(step, carry):
            begin = pl.multiple_of(step * GROUP, GROUP)
            qg = q_ref[pl.ds(begin, GROUP), :]
            sg = s_ref[pl.ds(begin, GROUP), :]
            for s in range(shapes_n):
                pick_ref[:, s * 128 : (s + 1) * 128] = jnp.where(sg == s, qg, jnp.zeros_like(qg))
            part = jnp.dot(pick_ref[...], w_ref[...], preferred_element_type=jnp.float32)
            high = part.astype(jnp.bfloat16)
            low = (part - high.astype(jnp.float32)).astype(jnp.bfloat16)
            cells = jnp.dot(high, r_ref[...], preferred_element_type=jnp.float32)
            cells = cells + jnp.dot(low, r_ref[...], preferred_element_type=jnp.float32)
            for du in range(3):
                tile_ref[pl.ds(du, GROUP, stride=4), :] = cells[:, du * 128 : (du + 1) * 128]

            def one_batch(batch, inner):
                first = begin + batch * BATCH
                clash = clash_ref[step * (GROUP // BATCH) + batch]
                rows = [base_ref[first + j] for j in range(BATCH)]
                at = [pl.multiple_of(batch * BATCH * 4, 8) + 4 * j for j in range(BATCH)]

                @pl.when(clash == 0)
                def _():
                    sums = [grid_ref[pl.ds(rows[j], 3), :] + tile_ref[pl.ds(at[j], 3), :] for j in range(BATCH)]
                    for j in range(BATCH):
                        grid_ref[pl.ds(rows[j], 3), :] = sums[j]

                @pl.when(clash != 0)
                def _():
                    for j in range(BATCH):
                        grid_ref[pl.ds(rows[j], 3), :] += tile_ref[pl.ds(at[j], 3), :]

                return inner

            return lax.fori_loop(0, GROUP // BATCH, one_batch, carry)

        lax.fori_loop(0, (live_ref[0] + GROUP - 1) // GROUP, one_group, 0)

    lane = lax.broadcasted_iota(jnp.int32, (8, 128), 1)
    zoff = lane // 8 % 8
    yoff = lane % 8
    next_k = lax.rem(k + 1, KZ)
    last_k = lax.rem(k + KZ - 1, KZ)

    def swap(value, bit):
        return jnp.where(lane // bit % 2 == 1, pltpu.roll(value, bit, 1), pltpu.roll(value, 128 - bit, 1))

    def combined(row, stride):
        def at(copy, plane, dv):
            start = (copy * KZ + plane) * PLANE + row + dv * UROWS
            if stride is None:
                return grid_ref[pl.ds(start, 8), :]
            return grid_ref[pl.ds(start, 8, stride=stride), :]

        def even(pv, dv):
            return jnp.where(zoff < 6, at(pv, k, dv), at(pv, next_k, dv))

        def odd(pv, dv):
            return jnp.where(zoff // 2 == 2, at(2 + pv, last_k, dv), at(2 + pv, k, dv))

        def along_y(get):
            straight = jnp.where(yoff < 6, get(0, 0), get(0, 1))
            crossed = jnp.where(yoff // 2 == 2, get(1, -1), get(1, 0))
            return straight + swap(crossed, 4)

        return along_y(even) + swap(along_y(odd), 32)

    def one_slab(v, top):
        row = (v + 1) * UROWS + 1
        begin = pl.multiple_of(v * 16, 16)
        for half in range(2):
            value = combined(row + 8 * half, None)
            plane_ref[pl.ds(begin + 8 * half, 8), :] = value
            top = jnp.maximum(top, jnp.abs(value))
        return top

    top = lax.fori_loop(0, VOUT, one_slab, jnp.zeros((8, 128), jnp.float32))
    line = lax.broadcasted_iota(jnp.int32, (8, 128), 0)
    for side in range(2):
        for c in range(5):
            value = combined((8 * c + 1) * UROWS + side * 17, UROWS)
            if c == 4:
                value = jnp.where(line < 2, value, 0.0)
            plane_ref[TAIL + side * 40 + c * 8 : TAIL + side * 40 + c * 8 + 8, :] = value
            top = jnp.maximum(top, jnp.abs(value))
    top = jnp.maximum(jnp.max(top, axis=0, keepdims=True), 1e-37)
    power = jnp.ceil(jnp.log2(top) * 16.0 + 0.01)
    shrink = jnp.exp2(power * -0.0625)
    last = plane_ref[SCALE_ROW - 2 : SCALE_ROW + 6, :]
    whole = jnp.round(plane_ref[...] * shrink * LEVELS)
    out_ref[0] = whole.astype(jnp.int32).astype(out_ref.dtype)
    marked = jnp.where(line == 2, power, jnp.round(last * shrink * LEVELS))
    both = jnp.concatenate([marked, jnp.round(plane_ref[SCALE_ROW + 6 : SCALE_ROW + 14, :] * shrink * LEVELS)], axis=0)
    out_ref[0, SCALE_ROW - 2 : SCALE_ROW + 14, :] = both.astype(jnp.int32).astype(out_ref.dtype)


def gather_kernel(x_ref, out_ref, edge_ref, tail_ref, turn_ref, grow_ref):
    step = pl.program_id(0)

    @pl.when(step == 0)
    def _():
        for src in range(16):
            tail = x_ref[src, TAIL:SENT, :].astype(jnp.float32)
            grow = jnp.exp2(tail[SCALE_ROW - TAIL : SCALE_ROW - TAIL + 1] * 0.0625) / LEVELS
            grow_ref[src * 8 : src * 8 + 8, :] = jnp.broadcast_to(grow, (8, 128))
            tail_ref[src * 80 : (src + 1) * 80, :] = tail * grow

    lane = lax.broadcasted_iota(jnp.int32, (8, 128), 1)
    line = lax.broadcasted_iota(jnp.int32, (8, 128), 0)
    first = jnp.where(step == 0, 0, 2 * step - 1)
    second = jnp.where(step == 0, VOUT - 1, 2 * step)
    for src in range(16):
        grow = grow_ref[src * 8 : src * 8 + 8, :]
        halves = []
        for v in (first, second):
            both = x_ref[src, pl.ds(pl.multiple_of(v * 16, 16), 16), :].astype(jnp.float32)
            above = tail_ref[pl.ds((src + 1) % 16 * 80 + v, 1), :]
            below = tail_ref[pl.ds((src + 15) % 16 * 80 + 40 + v, 1), :]
            upper = both[0:8] * grow + jnp.where(line == 0, below, 0.0)
            lower = both[8:16] * grow + jnp.where(line == 7, above, 0.0)
            halves.append((upper, lower))
        for half in range(2):
            da, db = halves[0][half], halves[1][half]
            begin = src * 32 + half * 16
            turn_ref[pl.ds(begin, 8, stride=2), :] = jnp.where(lane < 64, da, pltpu.roll(db, 64, 1))
            turn_ref[pl.ds(begin + 1, 8, stride=2), :] = jnp.where(lane < 64, pltpu.roll(da, 64, 1), db)

    def emit(store):
        for c in range(4):
            block = turn_ref[c * 128 : (c + 1) * 128, :].T.reshape(2, 8, 8, 128)
            store(c, block)

    @pl.when(step == 0)
    def _():
        def store(c, block):
            edge_ref[:, :, :, c * 128 : (c + 1) * 128] = block

        emit(store)

    @pl.when(step != 0)
    def _():
        def store(c, block):
            out_ref[:, 0:8, c * 128 : (c + 1) * 128] = block[0]
            out_ref[:, 8:16, c * 128 : (c + 1) * 128] = block[1]

        emit(store)


def from_behind(block, axis, distance):
    devices = range(lax.axis_size(axis))
    route = [((i - distance) % len(devices), i) for i in devices]
    return lax.ppermute(block, axis, route)


def on_device(charges, weight_tiles, block_shape, block_box, live_blocks):
    nblk, atoms = charges.shape
    shapes_n, _, cells = weight_tiles.shape
    wflat = weight_tiles.reshape(shapes_n * atoms, cells)
    slot = jnp.arange(nblk, dtype=jnp.int32)
    shape = jnp.where(slot < live_blocks[0], block_shape, shapes_n)
    shape = jnp.broadcast_to(shape.astype(jnp.bfloat16)[:, None], (nblk, 128))
    u = block_box // 2048
    v = block_box // 32 % 64
    w = block_box % 32
    copy = (w % 2) * 2 + v % 2
    base = (copy * KZ + w // 2) * PLANE + (v // 2 + 2) * UROWS + u
    batched = base.reshape(nblk // BATCH, BATCH).T
    near = jnp.abs(batched[:, None, :] - batched[None, :, :]) < 3
    order = np.arange(BATCH)[:, None] < np.arange(BATCH)[None, :]
    clash = jnp.any(near & order[:, :, None], axis=(0, 1)).astype(jnp.int32)

    whole = lambda shp: pl.BlockSpec(shp, lambda k, *_: (0,) * len(shp), pipeline_mode=pl.Buffered(1))
    sent = pl.pallas_call(
        spread_kernel,
        out_shape=jax.ShapeDtypeStruct((KZ, SENT, 128), WIRE),
        grid_spec=pltpu.PrefetchScalarGridSpec(
            num_scalar_prefetch=3,
            grid=(KZ,),
            in_specs=[whole((nblk, 128)), whole((nblk, 128)), whole((shapes_n * atoms, cells)), whole((512, 384))],
            out_specs=pl.BlockSpec((1, SENT, 128), lambda k, *_: (k, 0, 0)),
            scratch_shapes=[
                pltpu.VMEM((GROWS + SPARE, 128), jnp.float32),
                pltpu.VMEM((GROUP, shapes_n * atoms), jnp.bfloat16),
                pltpu.VMEM((GROUP * 4, 128), jnp.float32),
                pltpu.VMEM((SENT, 128), jnp.float32),
            ],
        ),
        compiler_params=pltpu.CompilerParams(vmem_limit_bytes=56 * 1024 * 1024),
        name="spread",
    )(base, clash, live_blocks, charges, shape, wflat, jnp.asarray(restriction(), jnp.bfloat16))
    got = lax.all_to_all(sent, "bx", split_axis=0, concat_axis=0, tiled=True)
    main, edge = pl.pallas_call(
        gather_kernel,
        out_shape=(
            jax.ShapeDtypeStruct((8, 256, 512), jnp.float32),
            jax.ShapeDtypeStruct((2, 8, 8, 512), jnp.float32),
        ),
        grid=(17,),
        in_specs=[pl.BlockSpec((KZ, SENT, 128), lambda p: (0, 0, 0), pipeline_mode=pl.Buffered(1))],
        out_specs=(
            pl.BlockSpec((8, 16, 512), lambda p: (0, jnp.maximum(p - 1, 0), 0)),
            pl.BlockSpec((2, 8, 8, 512), lambda p: (0, 0, 0, 0)),
        ),
        scratch_shapes=[pltpu.VMEM((16 * 80, 128), jnp.float32), pltpu.VMEM((512, 128), jnp.float32), pltpu.VMEM((128, 128), jnp.float32)],
        compiler_params=pltpu.CompilerParams(vmem_limit_bytes=40 * 1024 * 1024),
        name="gather",
    )(got)
    from_below = from_behind(edge[1], "by", 1)
    from_above = from_behind(edge[0], "by", -1)
    main = main.at[:, :8].add(from_below)
    return main.at[:, 248:].add(from_above)


def solution(mesh):
    return jax.shard_map(
        on_device,
        mesh=mesh,
        in_specs=(P(("bx", "by"), None), P(), P(("bx", "by")), P(("bx", "by")), P(("bx", "by"))),
        out_specs=P("bx", "by", None),
        check_vma=False,
    )
```

```python
import jax
import jax.numpy as jnp
import numpy as np
from jax import lax
from jax.experimental import pallas as pl
from jax.experimental.pallas import tpu as pltpu
from jax.sharding import PartitionSpec as P

NZ = 128
GROUP = 256
BATCH = 16
KZ = 16
UROWS = 24
VSLOTS = 33
FRONT = VSLOTS * UROWS
PLANE = UROWS * VSLOTS
GROWS = FRONT + 4 * KZ * PLANE
SPARE = -GROWS % 256 + 256
VOUT = 34
TAIL = VOUT * 16
SENT = TAIL + 80
WIRE = jnp.int16
LEVELS = 32700.0
UNROLL = 11
SCALE_ROW = TAIL + 34


def restriction():
    coef = [1.0, 4.0, 6.0, 4.0, 1.0]
    table = np.zeros((4, 512, 384), np.float32)
    for p in range(8):
        for mm in range(6):
            tap = p + 4 - 2 * mm
            if not 0 <= tap < 5:
                continue
            for q in range(8):
                for r in range(8):
                    for kind in range(4):
                        z = (r - 2 + 4 * (kind // 2)) % 8
                        y = (q - 2 + 4 * (kind % 2)) % 8
                        table[kind, (p * 8 + q) * 8 + r, mm // 2 * 128 + mm % 2 * 64 + z * 8 + y] = coef[tap] / 8.0
    return np.concatenate([table, table], axis=1).reshape(4096, 384)


def spread_kernel(base_ref, clash_ref, live_ref, q_ref, s_ref, w_ref, r_ref, out_ref, grid_ref, pick_ref, kind_ref, tile_ref, plane_ref):
    k = pl.program_id(0)
    shapes_n = w_ref.shape[0] // 128

    @pl.when(k == 0)
    def _():
        def clear(step, carry):
            grid_ref[pl.ds(pl.multiple_of(step * 256, 256), 256), :] = jnp.zeros((256, 128), jnp.float32)
            return carry

        lax.fori_loop(0, (GROWS + SPARE) // 256, clear, 0)

        def one_group(step, carry):
            begin = pl.multiple_of(step * GROUP, GROUP)
            qg = q_ref[pl.ds(begin, GROUP), :]
            code = s_ref[pl.ds(begin, GROUP), :].astype(jnp.float32)
            whole = jnp.floor(code * 0.25)
            sg = whole.astype(jnp.bfloat16)
            kind = code - 4.0 * whole
            for s in range(shapes_n):
                pick_ref[:, s * 128 : (s + 1) * 128] = jnp.where(sg == s, qg, jnp.zeros_like(qg))
            part = jnp.dot(pick_ref[...], w_ref[...], preferred_element_type=jnp.float32)
            high = part.astype(jnp.bfloat16)
            low = (part - high.astype(jnp.float32)).astype(jnp.bfloat16)
            both = jnp.concatenate([high, low], axis=1)
            kind = jnp.concatenate([kind.astype(jnp.bfloat16)] * 8, axis=1)
            for c in range(4):
                kind_ref[:, c * 1024 : (c + 1) * 1024] = jnp.where(kind == c, both, jnp.zeros_like(both))
            cells = jnp.dot(kind_ref[...], r_ref[...], preferred_element_type=jnp.float32)
            for du in range(3):
                tile_ref[pl.ds(du, GROUP, stride=4), :] = cells[:, du * 128 : (du + 1) * 128]

            def one_batch(batch, inner):
                first = begin + batch * BATCH
                clash = clash_ref[step * (GROUP // BATCH) + batch]
                rows = [base_ref[first + j] for j in range(BATCH)]
                at = [pl.multiple_of(batch * BATCH * 4, 8) + 4 * j for j in range(BATCH)]

                @pl.when(clash == 0)
                def _():
                    sums = [grid_ref[pl.ds(rows[j], 3), :] + tile_ref[pl.ds(at[j], 3), :] for j in range(BATCH)]
                    for j in range(BATCH):
                        grid_ref[pl.ds(rows[j], 3), :] = sums[j]

                @pl.when(clash != 0)
                def _():
                    for j in range(BATCH):
                        grid_ref[pl.ds(rows[j], 3), :] += tile_ref[pl.ds(at[j], 3), :]

                return inner

            return lax.fori_loop(0, GROUP // BATCH, one_batch, carry)

        lax.fori_loop(0, (live_ref[0] + GROUP - 1) // GROUP, one_group, 0)

    lane = lax.broadcasted_iota(jnp.int32, (8, 128), 1)
    z_kept = (lane & 56) < 48
    z_past = (lane & 56) < 16
    y_kept = (lane & 7) < 6
    y_past = (lane & 7) < 2
    next_k = lax.rem(k + 1, KZ)
    last_k = lax.rem(k + KZ - 1, KZ)

    def slab(odd, row, stride=None):
        def at(copy, plane):
            start = pl.multiple_of(FRONT + (copy * KZ + plane) * PLANE, 8) + row
            return grid_ref[pl.ds(start, 8, stride=stride), :]

        return jnp.where(z_kept, at(odd, k), at(odd, next_k)) + jnp.where(z_past, at(2 + odd, last_k), at(2 + odd, k))

    def put(row, value, top):
        plane_ref[pl.ds(row, 8), :] = value
        return jnp.maximum(top, jnp.abs(value))

    def one_slab(v, carry):
        top, evens, odds = carry
        new_evens, new_odds = [], []
        for half in range(2):
            row = pl.multiple_of(v * UROWS, 8) + 8 + 8 * half
            even, odd = slab(0, row), slab(1, row - UROWS)
            value = jnp.where(y_kept, evens[half], even) + jnp.where(y_past, odds[half], odd)
            place = jnp.where(v == 0, VOUT - 2, v - 1)
            top = put(pl.multiple_of(place * 16, 16) + 8 * half, value, top)
            new_evens.append(even)
            new_odds.append(odd)
        return top, tuple(new_evens), tuple(new_odds)

    zero = jnp.zeros((8, 128), jnp.float32)
    top, _, odds = lax.fori_loop(0, VOUT - 1, one_slab, (zero, (zero, zero), (zero, zero)), unroll=UNROLL)
    for half in range(2):
        top = put((VOUT - 1) * 16 + 8 * half, jnp.where(y_past, odds[half], 0.0), top)
    line = lax.broadcasted_iota(jnp.int32, (8, 128), 0)
    for side in range(2):
        for c in range(5):
            row = (8 * c - 1) * UROWS + 7 + side * 17
            even = jnp.where(y_kept, slab(0, row, UROWS), slab(0, row + UROWS, UROWS))
            odd = jnp.where(y_past, slab(1, row - UROWS, UROWS), slab(1, row, UROWS))
            if c == 0:
                odd = jnp.where(line > 0, odd, 0.0)
            if c == 4:
                even = jnp.where(line < 1, even, 0.0)
                odd = jnp.where(line < 2, odd, 0.0)
            top = put(TAIL + side * 40 + c * 8, even + odd, top)
    top = jnp.maximum(jnp.max(top, axis=0, keepdims=True), 1e-37)
    power = jnp.ceil(jnp.log2(top) * 16.0 + 0.01)
    shrink = jnp.exp2(power * -0.0625)
    last = plane_ref[SCALE_ROW - 2 : SCALE_ROW + 6, :]
    whole = jnp.round(plane_ref[...] * shrink * LEVELS)
    out_ref[0] = whole.astype(jnp.int32).astype(out_ref.dtype)
    marked = jnp.where(line == 2, power, jnp.round(last * shrink * LEVELS))
    both = jnp.concatenate([marked, jnp.round(plane_ref[SCALE_ROW + 6 : SCALE_ROW + 14, :] * shrink * LEVELS)], axis=0)
    out_ref[0, SCALE_ROW - 2 : SCALE_ROW + 14, :] = both.astype(jnp.int32).astype(out_ref.dtype)


def take_tails(tails, tail_ref, grow_ref):
    for src in range(16):
        tail = jnp.concatenate([t[src] for t in tails], axis=0).astype(jnp.float32)
        grow = jnp.exp2(tail[SCALE_ROW - TAIL : SCALE_ROW - TAIL + 1] * 0.0625) / LEVELS
        grow_ref[src * 8 : src * 8 + 8, :] = jnp.broadcast_to(grow, (8, 128))
        tail_ref[src * 80 : (src + 1) * 80, :] = tail * grow


def turn(rows_of, slabs, tail_ref, grow_ref, turn_ref):
    lane = lax.broadcasted_iota(jnp.int32, (8, 128), 1)
    line = lax.broadcasted_iota(jnp.int32, (8, 128), 0)
    for src in range(16):
        grow = grow_ref[src * 8 : src * 8 + 8, :]
        halves = []
        for which in range(2):
            both = rows_of(src, which).astype(jnp.float32)
            above = tail_ref[pl.ds((src + 1) % 16 * 80 + slabs[which], 1), :]
            below = tail_ref[pl.ds((src + 15) % 16 * 80 + 40 + slabs[which], 1), :]
            upper = both[0:8] * grow + jnp.where(line == 0, below, 0.0)
            lower = both[8:16] * grow + jnp.where(line == 7, above, 0.0)
            halves.append((upper, lower))
        for half in range(2):
            da, db = halves[0][half], halves[1][half]
            begin = src * 32 + half * 16
            turn_ref[pl.ds(begin, 8, stride=2), :] = jnp.where(lane < 64, da, pltpu.roll(db, 64, 1))
            turn_ref[pl.ds(begin + 1, 8, stride=2), :] = jnp.where(lane < 64, pltpu.roll(da, 64, 1), db)
    return [turn_ref[c * 128 : (c + 1) * 128, :].T.reshape(2, 8, 8, 128) for c in range(4)]


def edge_kernel(low_ref, high_ref, *refs):
    tails, (down_ref, up_ref), scratch = refs[:5], refs[5:7], refs[7:]
    take_tails(tails, *scratch[:2])
    blocks = turn(lambda src, which: (low_ref, high_ref)[which][src], (0, VOUT - 1), *scratch)
    for c, block in enumerate(blocks):
        down_ref[:, :, c * 128 : (c + 1) * 128] = block[0][:, 6:8]
        up_ref[:, :, c * 128 : (c + 1) * 128] = block[1][:, 0:2]


def inner_kernel(x_ref, *refs):
    tails, out_ref, scratch = refs[:5], refs[5], refs[6:]
    step = pl.program_id(0)

    @pl.when(step == 0)
    def _():
        take_tails(tails, *scratch[:2])

    slab = 2 * step + 3
    blocks = turn(lambda src, which: x_ref[src, which * 16 : which * 16 + 16, :], (slab, slab + 1), *scratch)
    for c, block in enumerate(blocks):
        out_ref[:, 0:8, c * 128 : (c + 1) * 128] = block[0]
        out_ref[:, 8:16, c * 128 : (c + 1) * 128] = block[1]


def outer_kernel(x_ref, *refs):
    tails, (below_ref, above_ref, _, out_ref), scratch = refs[:5], refs[5:9], refs[9:]
    step = pl.program_id(0)

    @pl.when(step == 0)
    def _():
        take_tails(tails, *scratch[:2])

    slab = 30 * step + 1
    blocks = turn(lambda src, which: x_ref[src, which * 16 : which * 16 + 16, :], (slab, slab + 1), *scratch)
    for c, block in enumerate(blocks):
        out_ref[:, 0:8, c * 128 : (c + 1) * 128] = block[0]
        out_ref[:, 8:16, c * 128 : (c + 1) * 128] = block[1]

    @pl.when(step == 0)
    def _():
        out_ref[:, 0:2, :] += below_ref[...]

    @pl.when(step == 1)
    def _():
        out_ref[:, 14:16, :] += above_ref[...]


def from_behind(block, axis, distance):
    devices = range(lax.axis_size(axis))
    route = [((i - distance) % len(devices), i) for i in devices]
    return lax.ppermute(block, axis, route)


def on_device(charges, weight_tiles, block_shape, block_box, live_blocks):
    nblk, atoms = charges.shape
    shapes_n, _, cells = weight_tiles.shape
    wflat = weight_tiles.reshape(shapes_n * atoms, cells)
    slot = jnp.arange(nblk, dtype=jnp.int32)
    u = block_box // 2048
    v = block_box // 32 % 64
    w = block_box % 32
    kind = (w % 2) * 2 + v % 2
    base = FRONT + (kind * KZ + w // 2) * PLANE + v // 2 * UROWS + 7 + u
    code = jnp.where(slot < live_blocks[0], block_shape, shapes_n) * 4 + kind
    code = jnp.broadcast_to(code.astype(jnp.bfloat16)[:, None], (nblk, 128))
    batched = base.reshape(nblk // BATCH, BATCH).T
    near = jnp.abs(batched[:, None, :] - batched[None, :, :]) < 3
    order = np.arange(BATCH)[:, None] < np.arange(BATCH)[None, :]
    clash = jnp.any(near & order[:, :, None], axis=(0, 1)).astype(jnp.int32)

    whole = lambda shp: pl.BlockSpec(shp, lambda k, *_: (0,) * len(shp), pipeline_mode=pl.Buffered(1))
    sent = pl.pallas_call(
        spread_kernel,
        out_shape=jax.ShapeDtypeStruct((KZ, SENT, 128), WIRE),
        grid_spec=pltpu.PrefetchScalarGridSpec(
            num_scalar_prefetch=3,
            grid=(KZ,),
            in_specs=[whole((nblk, 128)), whole((nblk, 128)), whole((shapes_n * atoms, cells)), whole((4096, 384))],
            out_specs=pl.BlockSpec((1, SENT, 128), lambda k, *_: (k, 0, 0)),
            scratch_shapes=[
                pltpu.VMEM((GROWS + SPARE, 128), jnp.float32),
                pltpu.VMEM((GROUP, shapes_n * atoms), jnp.bfloat16),
                pltpu.VMEM((GROUP, 4096), jnp.bfloat16),
                pltpu.VMEM((GROUP * 4, 128), jnp.float32),
                pltpu.VMEM((SENT, 128), jnp.float32),
            ],
        ),
        compiler_params=pltpu.CompilerParams(vmem_limit_bytes=56 * 1024 * 1024),
        name="spread",
    )(base, clash, live_blocks, charges, code, wflat, jnp.asarray(restriction(), jnp.bfloat16))
    got = lax.all_to_all(sent, "bx", split_axis=0, concat_axis=0, tiled=True)
    piece = lambda i: pl.BlockSpec((KZ, 16, 128), lambda p: (0, i, 0))
    tails = [piece(TAIL // 16 + i) for i in range(5)]
    small = pl.BlockSpec((8, 2, 512), lambda p: (0, 0, 0))
    full = jax.ShapeDtypeStruct((8, 256, 512), jnp.float32)
    scratch = [
        pltpu.VMEM((16 * 80, 128), jnp.float32),
        pltpu.VMEM((128, 128), jnp.float32),
        pltpu.VMEM((512, 128), jnp.float32),
    ]
    params = pltpu.CompilerParams(vmem_limit_bytes=40 * 1024 * 1024)
    down, up = pl.pallas_call(
        edge_kernel,
        out_shape=(jax.ShapeDtypeStruct((8, 2, 512), jnp.float32),) * 2,
        grid=(1,),
        in_specs=[piece(VOUT - 2), piece(VOUT - 1)] + tails,
        out_specs=(small, small),
        scratch_shapes=scratch,
        compiler_params=params,
        name="edge",
    )(*[got] * 7)
    below = from_behind(up, "by", 1)
    above = from_behind(down, "by", -1)
    inner = pl.pallas_call(
        inner_kernel,
        out_shape=full,
        grid=(14,),
        in_specs=[pl.BlockSpec((KZ, 32, 128), lambda p: (0, p + 1, 0))] + tails,
        out_specs=pl.BlockSpec((8, 16, 512), lambda p: (0, p + 1, 0)),
        scratch_shapes=scratch,
        compiler_params=params,
        name="inner",
    )(*[got] * 6)
    return pl.pallas_call(
        outer_kernel,
        out_shape=full,
        grid=(2,),
        in_specs=[pl.BlockSpec((KZ, 32, 128), lambda p: (0, 15 * p, 0))]
        + tails
        + [small, small, pl.BlockSpec(memory_space=pl.ANY)],
        out_specs=pl.BlockSpec((8, 16, 512), lambda p: (0, 15 * p, 0)),
        scratch_shapes=scratch,
        input_output_aliases={8: 0},
        compiler_params=params,
        name="outer",
    )(*[got] * 6, below, above, inner)


def solution(mesh):
    return jax.shard_map(
        on_device,
        mesh=mesh,
        in_specs=(P(("bx", "by"), None), P(), P(("bx", "by")), P(("bx", "by")), P(("bx", "by"))),
        out_specs=P("bx", "by", None),
        check_vma=False,
    )
```

```python
import jax
import jax.numpy as jnp
import numpy as np
from jax import lax
from jax.experimental import pallas as pl
from jax.experimental.pallas import tpu as pltpu
from jax.sharding import PartitionSpec as P

NZ = 128
GROUP = 256
BATCH = 16
KZ = 16
UROWS = 24
VSLOTS = 33
FRONT = VSLOTS * UROWS
PLANE = UROWS * VSLOTS
GROWS = FRONT + 4 * KZ * PLANE
SPARE = -GROWS % 256 + 256
DUMP = GROWS + SPARE - 8
VOUT = 34
TAIL = VOUT * 16
SENT = TAIL + 80
WIRE = jnp.int16
LEVELS = 32700.0
UNROLL = 11
SCALE_ROW = TAIL + 34


def restriction():
    coef = [1.0, 4.0, 6.0, 4.0, 1.0]
    table = np.zeros((2, 512, 384), np.float32)
    for p in range(8):
        for mm in range(6):
            tap = p + 4 - 2 * mm
            if not 0 <= tap < 5:
                continue
            for q in range(8):
                for r in range(8):
                    z = (r - 2) % 8
                    for odd in range(2):
                        y = (q - 2 + 4 * odd) % 8
                        lane = z // 4 * 64 + mm % 2 * 32 + z % 4 * 8 + y
                        table[odd, (p * 8 + q) * 8 + r, mm // 2 * 128 + lane] = coef[tap] / 8.0
    return np.concatenate([table, table], axis=1).reshape(2048, 384)


def spread_kernel(base_ref, fast_ref, clash_ref, live_ref, q_ref, code_ref, w_any, r_any, out_ref, *scratch):
    grid_ref, w_ref, r_ref, pick_ref, kind_ref, tile_a, tile_b, plane_ref, sems = scratch
    shapes_n = w_ref.shape[0] // 128
    w_copy = pltpu.make_async_copy(w_any, w_ref, sems.at[0])
    r_copy = pltpu.make_async_copy(r_any, r_ref, sems.at[1])
    w_copy.start()
    r_copy.start()
    tile_b[...] = jnp.zeros(tile_b.shape, jnp.float32)

    def clear(step, carry):
        grid_ref[pl.ds(pl.multiple_of(step * 256, 256), 256), :] = jnp.zeros((256, 128), jnp.float32)
        return carry

    lax.fori_loop(0, (GROWS + SPARE) // 256, clear, 0)
    w_copy.wait()
    r_copy.wait()

    def product(step, tile_ref):
        begin = pl.multiple_of(step * GROUP, GROUP)
        qg = q_ref[pl.ds(begin, GROUP), :]
        codes = [code_ref[pl.ds(step * (GROUP // 128) + h, 1), :] for h in range(GROUP // 128)]
        code = jnp.concatenate([jnp.broadcast_to(c, (128, 128)).T for c in codes], axis=0)
        whole = jnp.floor(code * 0.25)
        sg = whole.astype(jnp.bfloat16)
        kind = code - 4.0 * whole
        z_odd = kind >= 2.0
        y_odd = jnp.where(z_odd, kind - 2.0, kind).astype(jnp.bfloat16)
        for s in range(shapes_n):
            pick_ref[:, s * 128 : (s + 1) * 128] = jnp.where(sg == s, qg, jnp.zeros_like(qg))
        part = jnp.dot(pick_ref[...], w_ref[...], preferred_element_type=jnp.float32)
        high = part.astype(jnp.bfloat16)
        low = (part - high.astype(jnp.float32)).astype(jnp.bfloat16)
        both = jnp.concatenate([high, low], axis=1)
        y_odd = jnp.concatenate([y_odd] * 8, axis=1)
        for c in range(2):
            kind_ref[:, c * 1024 : (c + 1) * 1024] = jnp.where(y_odd == c, both, jnp.zeros_like(both))
        cells = jnp.dot(kind_ref[...], r_ref[...], preferred_element_type=jnp.float32)
        for du in range(3):
            rows = cells[:, du * 128 : (du + 1) * 128]
            tile_ref[pl.ds(du, GROUP, stride=4), :] = jnp.where(z_odd, pltpu.roll(rows, 64, 1), rows)

    def deposit(step, tile_ref):
        for batch in range(GROUP // BATCH):
            first = step * GROUP + batch * BATCH
            rows = [fast_ref[first + j] for j in range(BATCH)]
            at = [(batch * BATCH + j) * 4 for j in range(BATCH)]
            sums = [grid_ref[pl.ds(rows[j], 3), :] + tile_ref[at[j] : at[j] + 3, :] for j in range(BATCH)]
            for j in range(BATCH):
                grid_ref[pl.ds(rows[j], 3), :] = sums[j]

    def deposit_rest(step, tile_ref):
        flag = clash_ref[step * (GROUP // BATCH)]
        for batch in range(1, GROUP // BATCH):
            flag = flag | clash_ref[step * (GROUP // BATCH) + batch]

        @pl.when(flag != 0)
        def _():
            def one_batch(batch, carry):
                @pl.when(clash_ref[step * (GROUP // BATCH) + batch] != 0)
                def _():
                    def one_block(j, inner):
                        slot = step * GROUP + batch * BATCH + j

                        @pl.when(fast_ref[slot] != base_ref[slot])
                        def _():
                            tile = tile_ref[pl.ds((batch * BATCH + j) * 4, 3), :]
                            grid_ref[pl.ds(base_ref[slot], 3), :] += tile

                        return inner

                    lax.fori_loop(0, BATCH, one_block, 0)

                return carry

            lax.fori_loop(0, GROUP // BATCH, one_batch, 0)

    def two_groups(pair, carry):
        before = jnp.maximum(2 * pair - 1, 0)
        product(2 * pair, tile_a)
        deposit(before, tile_b)

        @pl.when(pair > 0)
        def _():
            deposit_rest(before, tile_b)

        product(2 * pair + 1, tile_b)
        deposit(2 * pair, tile_a)
        deposit_rest(2 * pair, tile_a)
        return carry

    pairs = (live_ref[0] + 2 * GROUP - 1) // (2 * GROUP)
    lax.fori_loop(0, pairs, two_groups, 0)
    deposit(2 * pairs - 1, tile_b)
    deposit_rest(2 * pairs - 1, tile_b)

    def one_plane(k, carry):
        combine(k, grid_ref, plane_ref, out_ref)
        return carry

    lax.fori_loop(0, KZ, one_plane, 0)


def combine(k, grid_ref, plane_ref, out_ref):
    lane = lax.broadcasted_iota(jnp.int32, (8, 128), 1)
    z = ((lane >> 6) << 2) + ((lane >> 3) & 3)
    z_kept = z < 6
    z_past = z < 2
    y_kept = (lane & 7) < 6
    y_past = (lane & 7) < 2
    next_k = lax.rem(k + 1, KZ)
    last_k = lax.rem(k + KZ - 1, KZ)

    def slab(odd, row, stride=None):
        def at(copy, plane):
            start = pl.multiple_of(FRONT + (copy * KZ + plane) * PLANE, 8) + row
            return grid_ref[pl.ds(start, 8, stride=stride), :]

        return jnp.where(z_kept, at(odd, k), at(odd, next_k)) + jnp.where(z_past, at(2 + odd, last_k), at(2 + odd, k))

    def put(row, value, top):
        plane_ref[pl.ds(row, 8), :] = value
        return jnp.maximum(top, jnp.abs(value))

    def one_slab(v, carry):
        top, evens, odds = carry
        new_evens, new_odds = [], []
        for half in range(2):
            row = pl.multiple_of(v * UROWS, 8) + 8 + 8 * half
            even, odd = slab(0, row), slab(1, row - UROWS)
            value = jnp.where(y_kept, evens[half], even) + jnp.where(y_past, odds[half], odd)
            place = jnp.where(v == 0, VOUT - 2, v - 1)
            top = put(pl.multiple_of(place * 16, 16) + 8 * half, value, top)
            new_evens.append(even)
            new_odds.append(odd)
        return top, tuple(new_evens), tuple(new_odds)

    zero = jnp.zeros((8, 128), jnp.float32)
    top, _, odds = lax.fori_loop(0, VOUT - 1, one_slab, (zero, (zero, zero), (zero, zero)), unroll=UNROLL)
    for half in range(2):
        top = put((VOUT - 1) * 16 + 8 * half, jnp.where(y_past, odds[half], 0.0), top)
    line = lax.broadcasted_iota(jnp.int32, (8, 128), 0)
    for side in range(2):
        for c in range(5):
            row = (8 * c - 1) * UROWS + 7 + side * 17
            even = jnp.where(y_kept, slab(0, row, UROWS), slab(0, row + UROWS, UROWS))
            odd = jnp.where(y_past, slab(1, row - UROWS, UROWS), slab(1, row, UROWS))
            if c == 0:
                odd = jnp.where(line > 0, odd, 0.0)
            if c == 4:
                even = jnp.where(line < 1, even, 0.0)
                odd = jnp.where(line < 2, odd, 0.0)
            top = put(TAIL + side * 40 + c * 8, even + odd, top)
    top = jnp.maximum(jnp.max(top, axis=0, keepdims=True), 1e-37)
    power = jnp.ceil(jnp.log2(top) * 16.0 + 0.01)
    shrink = jnp.exp2(power * -0.0625)
    last = plane_ref[SCALE_ROW - 2 : SCALE_ROW + 6, :]
    whole = jnp.round(plane_ref[...] * shrink * LEVELS)
    out_ref[k] = whole.astype(jnp.int32).astype(out_ref.dtype)
    marked = jnp.where(line == 2, power, jnp.round(last * shrink * LEVELS))
    both = jnp.concatenate([marked, jnp.round(plane_ref[SCALE_ROW + 6 : SCALE_ROW + 14, :] * shrink * LEVELS)], axis=0)
    out_ref[k, SCALE_ROW - 2 : SCALE_ROW + 14, :] = both.astype(jnp.int32).astype(out_ref.dtype)


def take_tails(tails, tail_ref, grow_ref):
    for src in range(16):
        tail = jnp.concatenate([t[src] for t in tails], axis=0).astype(jnp.float32)
        grow = jnp.exp2(tail[SCALE_ROW - TAIL : SCALE_ROW - TAIL + 1] * 0.0625) / LEVELS
        grow_ref[src * 8 : src * 8 + 8, :] = jnp.broadcast_to(grow, (8, 128))
        tail_ref[src * 80 : (src + 1) * 80, :] = tail * grow


def turn(rows_of, slabs, tail_ref, grow_ref, turn_ref):
    lane = lax.broadcasted_iota(jnp.int32, (8, 128), 1)
    line = lax.broadcasted_iota(jnp.int32, (8, 128), 0)
    for src in range(16):
        grow = grow_ref[src * 8 : src * 8 + 8, :]
        halves = []
        for which in range(2):
            both = rows_of(src, which).astype(jnp.float32)
            above = tail_ref[pl.ds((src + 1) % 16 * 80 + slabs[which], 1), :]
            below = tail_ref[pl.ds((src + 15) % 16 * 80 + 40 + slabs[which], 1), :]
            upper = both[0:8] * grow + jnp.where(line == 0, below, 0.0)
            lower = both[8:16] * grow + jnp.where(line == 7, above, 0.0)
            halves.append((upper, lower))
        for half in range(2):
            da, db = halves[0][half], halves[1][half]
            begin = src * 32 + half * 16
            turn_ref[pl.ds(begin, 8, stride=2), :] = jnp.where(lane & 32 == 0, da, pltpu.roll(db, 32, 1))
            turn_ref[pl.ds(begin + 1, 8, stride=2), :] = jnp.where(lane & 32 == 0, pltpu.roll(da, 96, 1), db)
    blocks = []
    for c in range(4):
        block = turn_ref[c * 128 : (c + 1) * 128, :].T.reshape(2, 2, 4, 8, 128)
        blocks.append([jnp.concatenate([block[0, which], block[1, which]], axis=0) for which in range(2)])
    return blocks


def edge_kernel(low_ref, high_ref, *refs):
    tails, (down_ref, up_ref), scratch = refs[:5], refs[5:7], refs[7:]
    take_tails(tails, *scratch[:2])
    blocks = turn(lambda src, which: (low_ref, high_ref)[which][src], (0, VOUT - 1), *scratch)
    for c, block in enumerate(blocks):
        down_ref[:, :, c * 128 : (c + 1) * 128] = block[0][:, 6:8]
        up_ref[:, :, c * 128 : (c + 1) * 128] = block[1][:, 0:2]


def inner_kernel(x_ref, *refs):
    tails, out_ref, scratch = refs[:5], refs[5], refs[6:]
    step = pl.program_id(0)

    @pl.when(step == 0)
    def _():
        take_tails(tails, *scratch[:2])

    slab = 2 * step + 3
    blocks = turn(lambda src, which: x_ref[src, which * 16 : which * 16 + 16, :], (slab, slab + 1), *scratch)
    for c, block in enumerate(blocks):
        out_ref[:, 0:8, c * 128 : (c + 1) * 128] = block[0]
        out_ref[:, 8:16, c * 128 : (c + 1) * 128] = block[1]


def outer_kernel(x_ref, *refs):
    tails, (below_ref, above_ref, _, out_ref), scratch = refs[:5], refs[5:9], refs[9:]
    step = pl.program_id(0)

    @pl.when(step == 0)
    def _():
        take_tails(tails, *scratch[:2])

    slab = 30 * step + 1
    blocks = turn(lambda src, which: x_ref[src, which * 16 : which * 16 + 16, :], (slab, slab + 1), *scratch)
    for c, block in enumerate(blocks):
        out_ref[:, 0:8, c * 128 : (c + 1) * 128] = block[0]
        out_ref[:, 8:16, c * 128 : (c + 1) * 128] = block[1]

    @pl.when(step == 0)
    def _():
        out_ref[:, 0:2, :] += below_ref[...]

    @pl.when(step == 1)
    def _():
        out_ref[:, 14:16, :] += above_ref[...]


def from_behind(block, axis, distance):
    devices = range(lax.axis_size(axis))
    route = [((i - distance) % len(devices), i) for i in devices]
    return lax.ppermute(block, axis, route)


def on_device(charges, weight_tiles, block_shape, block_box, live_blocks):
    nblk, atoms = charges.shape
    shapes_n, _, cells = weight_tiles.shape
    wflat = weight_tiles.reshape(shapes_n * atoms, cells)
    slot = jnp.arange(nblk, dtype=jnp.int32)
    u = block_box // 2048
    v = block_box // 32 % 64
    w = block_box % 32
    kind = (w % 2) * 2 + v % 2
    base = FRONT + (kind * KZ + w // 2) * PLANE + v // 2 * UROWS + 7 + u
    code = jnp.where(slot < live_blocks[0], block_shape, shapes_n) * 4 + kind
    code = code.astype(jnp.float32).reshape(nblk // 128, 128)
    batched = base.reshape(nblk // BATCH, BATCH).T
    near = jnp.abs(batched[:, None, :] - batched[None, :, :]) < 3
    earlier = np.arange(BATCH)[:, None] < np.arange(BATCH)[None, :]
    late = jnp.any(near & earlier[:, :, None], axis=0)
    fast = jnp.where(late, DUMP, batched).T.reshape(nblk)
    clash = jnp.any(late, axis=0).astype(jnp.int32)

    vmem = pl.BlockSpec(memory_space=pltpu.VMEM)
    smem = pl.BlockSpec(memory_space=pltpu.SMEM)
    hbm = pl.BlockSpec(memory_space=pl.ANY)
    sent = pl.pallas_call(
        spread_kernel,
        out_shape=jax.ShapeDtypeStruct((KZ, SENT, 128), WIRE),
        in_specs=[smem] * 4 + [vmem] * 2 + [hbm] * 2,
        out_specs=vmem,
        scratch_shapes=[
            pltpu.VMEM((GROWS + SPARE, 128), jnp.float32),
            pltpu.VMEM((shapes_n * atoms, cells), jnp.bfloat16),
            pltpu.VMEM((2048, 384), jnp.bfloat16),
            pltpu.VMEM((GROUP, shapes_n * atoms), jnp.bfloat16),
            pltpu.VMEM((GROUP, 2048), jnp.bfloat16),
            pltpu.VMEM((GROUP * 4, 128), jnp.float32),
            pltpu.VMEM((GROUP * 4, 128), jnp.float32),
            pltpu.VMEM((SENT, 128), jnp.float32),
            pltpu.SemaphoreType.DMA((2,)),
        ],
        compiler_params=pltpu.CompilerParams(vmem_limit_bytes=56 * 1024 * 1024),
        name="spread",
    )(base, fast, clash, live_blocks, charges, code, wflat, jnp.asarray(restriction(), jnp.bfloat16))
    got = lax.all_to_all(sent, "bx", split_axis=0, concat_axis=0, tiled=True)
    piece = lambda i: pl.BlockSpec((KZ, 16, 128), lambda p: (0, i, 0))
    tails = [piece(TAIL // 16 + i) for i in range(5)]
    small = pl.BlockSpec((8, 2, 512), lambda p: (0, 0, 0))
    full = jax.ShapeDtypeStruct((8, 256, 512), jnp.float32)
    scratch = [
        pltpu.VMEM((16 * 80, 128), jnp.float32),
        pltpu.VMEM((128, 128), jnp.float32),
        pltpu.VMEM((512, 128), jnp.float32),
    ]
    params = pltpu.CompilerParams(vmem_limit_bytes=40 * 1024 * 1024)
    down, up = pl.pallas_call(
        edge_kernel,
        out_shape=(jax.ShapeDtypeStruct((8, 2, 512), jnp.float32),) * 2,
        grid=(1,),
        in_specs=[piece(VOUT - 2), piece(VOUT - 1)] + tails,
        out_specs=(small, small),
        scratch_shapes=scratch,
        compiler_params=params,
        name="edge",
    )(*[got] * 7)
    below = from_behind(up, "by", 1)
    above = from_behind(down, "by", -1)
    inner = pl.pallas_call(
        inner_kernel,
        out_shape=full,
        grid=(14,),
        in_specs=[pl.BlockSpec((KZ, 32, 128), lambda p: (0, p + 1, 0))] + tails,
        out_specs=pl.BlockSpec((8, 16, 512), lambda p: (0, p + 1, 0)),
        scratch_shapes=scratch,
        compiler_params=params,
        name="inner",
    )(*[got] * 6)
    return pl.pallas_call(
        outer_kernel,
        out_shape=full,
        grid=(2,),
        in_specs=[pl.BlockSpec((KZ, 32, 128), lambda p: (0, 15 * p, 0))]
        + tails
        + [small, small, pl.BlockSpec(memory_space=pl.ANY)],
        out_specs=pl.BlockSpec((8, 16, 512), lambda p: (0, 15 * p, 0)),
        scratch_shapes=scratch,
        input_output_aliases={8: 0},
        compiler_params=params,
        name="outer",
    )(*[got] * 6, below, above, inner)


def solution(mesh):
    return jax.shard_map(
        on_device,
        mesh=mesh,
        in_specs=(P(("bx", "by"), None), P(), P(("bx", "by")), P(("bx", "by")), P(("bx", "by"))),
        out_specs=P("bx", "by", None),
        check_vma=False,
    )
```

```python
import jax
import jax.numpy as jnp
import numpy as np
from jax import lax
from jax.experimental import pallas as pl
from jax.experimental.pallas import tpu as pltpu
from jax.sharding import PartitionSpec as P

NZ = 128
GROUP = 256
BATCH = 16
KZ = 16
UROWS = 24
VSLOTS = 34
FRONT = VSLOTS * UROWS
PLANE = UROWS * VSLOTS
GROWS = FRONT + 4 * KZ * PLANE
SPARE = -GROWS % 256 + 256
DUMP = GROWS + SPARE - 8
VOUT = 34
TAIL = VOUT * 16
SENT = TAIL + 80
WIRE = jnp.int16
LEVELS = 32700.0
UNROLL = 11
SCALE_ROW = TAIL + 34


def restriction():
    coef = [1.0, 4.0, 6.0, 4.0, 1.0]
    table = np.zeros((512, 384), np.float32)
    for p in range(8):
        for mm in range(6):
            tap = p + 4 - 2 * mm
            if not 0 <= tap < 5:
                continue
            for q in range(8):
                for r in range(8):
                    z, y = (r - 2) % 8, (q - 2) % 8
                    lane = z // 4 * 64 + mm % 2 * 32 + z % 4 * 8 + y
                    table[(p * 8 + q) * 8 + r, mm // 2 * 128 + lane] = coef[tap] / 8.0
    return np.concatenate([table, table], axis=0)


def place_blocks(shape_ref, box_ref, live, base_ref, fast_ref, flag_ref, code_ref):
    lane = lax.broadcasted_iota(jnp.int32, base_ref.shape, 1)
    slot = lax.broadcasted_iota(jnp.int32, base_ref.shape, 0) * 128 + lane
    box = box_ref[...]
    u = box >> 11
    v = (box >> 5) & 63
    w = box & 31
    kind = (w & 1) * 2 + (v & 1)
    base = FRONT + (kind * KZ + (w >> 1)) * PLANE + (v >> 1) * UROWS + 7 + u
    late = jnp.zeros(base.shape, jnp.int32)
    for d in range(1, BATCH):
        near = jnp.abs(base - pltpu.roll(base, d, 1)) < 3
        late = jnp.where(near & ((lane & (BATCH - 1)) >= d), 1, late)
    base_ref[...] = base
    fast_ref[...] = jnp.where(late == 1, DUMP, base)
    for d in (1, 2, 4, 8):
        late = late | pltpu.roll(late, 128 - d, 1)
    flag_ref[...] = late
    code = jnp.where(slot < live, shape_ref[...], 32) * 4 + kind
    code_ref[...] = code.astype(jnp.float32)


def spread_kernel(live_ref, q_ref, shape_ref, box_ref, w_any, r_any, out_ref, *scratch):
    grid_ref, w_ref, r_ref, pick_ref, half_a, half_b, kind_a, kind_b, tile_a, tile_b, plane_ref = scratch[:11]
    base_v, fast_v, flag_v, code_ref, base_ref, fast_ref, flag_ref, sems = scratch[11:]
    shapes_n = w_ref.shape[0] // 128
    copies = [pltpu.make_async_copy(w_any, w_ref, sems.at[0]), pltpu.make_async_copy(r_any, r_ref, sems.at[1])]
    for copy in copies:
        copy.start()
    place_blocks(shape_ref, box_ref, live_ref[0], base_v, fast_v, flag_v, code_ref)
    for i, (here, there) in enumerate(((base_v, base_ref), (fast_v, fast_ref), (flag_v, flag_ref))):
        copies.append(pltpu.make_async_copy(here, there, sems.at[2 + i]))
        copies[-1].start()
    for ref in (half_b, kind_b, tile_a):
        ref[...] = jnp.zeros(ref.shape, ref.dtype)

    def clear(step, carry):
        grid_ref[pl.ds(pl.multiple_of(step * 256, 256), 256), :] = jnp.zeros((256, 128), jnp.float32)
        return carry

    lax.fori_loop(0, (GROWS + SPARE) // 256, clear, 0)
    for copy in copies:
        copy.wait()

    def product(step, half_ref, kind_ref):
        begin = pl.multiple_of(step * GROUP, GROUP)
        qg = q_ref[pl.ds(begin, GROUP), :]
        codes = [code_ref[pl.ds(step * (GROUP // 128) + h, 1), :] for h in range(GROUP // 128)]
        code = jnp.concatenate([jnp.broadcast_to(c, (128, 128)).T for c in codes], axis=0)
        whole = jnp.floor(code * 0.25)
        sg = whole.astype(jnp.bfloat16)
        kind_ref[...] = code - 4.0 * whole
        for s in range(shapes_n):
            pick_ref[:, s * 128 : (s + 1) * 128] = jnp.where(sg == s, qg, jnp.zeros_like(qg))
        part = jnp.dot(pick_ref[...], w_ref[...], preferred_element_type=jnp.float32)
        high = part.astype(jnp.bfloat16)
        half_ref[:, :512] = high
        half_ref[:, 512:] = (part - high.astype(jnp.float32)).astype(jnp.bfloat16)

    def arrange(half_ref, kind_ref, tile_ref):
        cells = jnp.dot(half_ref[...], r_ref[...], preferred_element_type=jnp.float32)
        kind = kind_ref[...]
        z_odd = kind >= 2.0
        y_odd = (kind == 1.0) | (kind == 3.0)
        y_upper = (lax.broadcasted_iota(jnp.int32, kind.shape, 1) & 4) != 0
        for du in range(3):
            rows = cells[:, du * 128 : (du + 1) * 128]
            rows = jnp.where(z_odd, pltpu.roll(rows, 64, 1), rows)
            crossed = jnp.where(y_upper, pltpu.roll(rows, 4, 1), pltpu.roll(rows, 124, 1))
            tile_ref[pl.ds(du, GROUP, stride=4), :] = jnp.where(y_odd, crossed, rows)

    def at(ref, step, i):
        return ref[step * (GROUP // 128) + i // 128, i % 128]

    def deposit(step, tile_ref):
        for batch in range(GROUP // BATCH):
            slots = [batch * BATCH + j for j in range(BATCH)]
            rows = [at(fast_ref, step, i) for i in slots]
            sums = [grid_ref[pl.ds(r, 3), :] + tile_ref[4 * i : 4 * i + 3, :] for r, i in zip(rows, slots)]
            for r, value in zip(rows, sums):
                grid_ref[pl.ds(r, 3), :] = value

    def deposit_rest(step, tile_ref):
        flag = at(flag_ref, step, 0)
        for batch in range(1, GROUP // BATCH):
            flag = flag | at(flag_ref, step, batch * BATCH)

        @pl.when(flag != 0)
        def _():
            def one_batch(batch, carry):
                row = step * (GROUP // 128) + batch // (128 // BATCH)
                head = batch % (128 // BATCH) * BATCH

                @pl.when(flag_ref[row, head] != 0)
                def _():
                    def one_block(j, inner):
                        spot = base_ref[row, head + j]

                        @pl.when(fast_ref[row, head + j] != spot)
                        def _():
                            grid_ref[pl.ds(spot, 3), :] += tile_ref[pl.ds((batch * BATCH + j) * 4, 3), :]

                        return inner

                    lax.fori_loop(0, BATCH, one_block, 0)

                return carry

            lax.fori_loop(0, GROUP // BATCH, one_batch, 0)

    def two_groups(pair, carry):
        step = 2 * pair
        product(step, half_a, kind_a)
        arrange(half_b, kind_b, tile_b)
        deposit(jnp.maximum(step - 2, 0), tile_a)
        product(step + 1, half_b, kind_b)
        arrange(half_a, kind_a, tile_a)
        deposit(jnp.maximum(step - 1, 0), tile_b)

        @pl.when(pair > 0)
        def _():
            deposit_rest(step - 1, tile_b)

        deposit_rest(step, tile_a)
        return carry

    pairs = (live_ref[0] + 2 * GROUP - 1) // (2 * GROUP)
    lax.fori_loop(0, pairs, two_groups, 0)
    arrange(half_b, kind_b, tile_b)
    deposit(2 * pairs - 2, tile_a)
    deposit(2 * pairs - 1, tile_b)
    deposit_rest(2 * pairs - 1, tile_b)

    def one_plane(k, carry):
        combine(k, grid_ref, plane_ref, out_ref)
        return carry

    lax.fori_loop(0, KZ, one_plane, 0)


def combine(k, grid_ref, plane_ref, out_ref):
    lane = lax.broadcasted_iota(jnp.int32, (8, 128), 1)
    z = ((lane >> 6) << 2) + ((lane >> 3) & 3)
    z_kept = z < 6
    z_past = z < 2
    y_kept = (lane & 7) < 6
    y_past = (lane & 7) < 2
    next_k = lax.rem(k + 1, KZ)
    last_k = lax.rem(k + KZ - 1, KZ)

    def slab(odd, row):
        def at(copy, plane):
            return grid_ref[pl.ds(pl.multiple_of(FRONT + (copy * KZ + plane) * PLANE + row, 8), 8), :]

        return jnp.where(z_kept, at(odd, k), at(odd, next_k)) + jnp.where(z_past, at(2 + odd, last_k), at(2 + odd, k))

    def put(row, value, top):
        plane_ref[pl.ds(row, 8), :] = value
        return jnp.maximum(top, jnp.abs(value))

    def put_ends(v, value, top):
        plane_ref[pl.ds(TAIL + v, 1), :] = value[7:8]
        plane_ref[pl.ds(TAIL + 39 + v, 1), :] = value[0:1]
        return jnp.maximum(top, jnp.abs(value))

    def one_slab(v, carry):
        top, evens, odds = carry
        new_evens, new_odds = [], []
        for part in range(3):
            row = v * UROWS + 8 * part
            even, odd = slab(0, row), slab(1, row - UROWS)
            value = jnp.where(y_kept, evens[part], even) + jnp.where(y_past, odds[part], odd)
            if part == 0:
                top = put_ends(v, value, top)
            else:
                place = jnp.where(v == 0, VOUT - 2, v - 1)
                top = put(pl.multiple_of(place * 16 + 8 * part - 8, 8), value, top)
            new_evens.append(even)
            new_odds.append(odd)
        return top, tuple(new_evens), tuple(new_odds)

    zero = jnp.zeros((8, 128), jnp.float32)
    top, evens, odds = lax.fori_loop(0, VOUT - 1, one_slab, (zero, (zero,) * 3, (zero,) * 3), unroll=UNROLL)
    for part in (1, 2):
        top = put((VOUT - 1) * 16 + 8 * part - 8, jnp.where(y_past, odds[part], 0.0), top)
    odd = slab(1, 32 * UROWS)
    top = put_ends(33, jnp.where(y_kept, evens[0], 0.0) + jnp.where(y_past, odds[0], odd), top)
    value = jnp.where(y_past, odd, 0.0)
    plane_ref[TAIL + 73 : TAIL + 74, :] = value[0:1]
    top = jnp.maximum(top, jnp.abs(value))
    line = lax.broadcasted_iota(jnp.int32, (8, 128), 0)
    top = jnp.maximum(jnp.max(top, axis=0, keepdims=True), 1e-37)
    power = jnp.ceil(jnp.log2(top) * 16.0 + 0.01)
    shrink = jnp.exp2(power * -0.0625)
    last = plane_ref[SCALE_ROW - 2 : SCALE_ROW + 6, :]
    whole = jnp.round(plane_ref[...] * shrink * LEVELS)
    out_ref[k] = whole.astype(jnp.int32).astype(out_ref.dtype)
    marked = jnp.where(line == 2, power, jnp.round(last * shrink * LEVELS))
    both = jnp.concatenate([marked, jnp.round(plane_ref[SCALE_ROW + 6 : SCALE_ROW + 14, :] * shrink * LEVELS)], axis=0)
    out_ref[k, SCALE_ROW - 2 : SCALE_ROW + 14, :] = both.astype(jnp.int32).astype(out_ref.dtype)


def take_tails(tails, tail_ref, grow_ref):
    for src in range(16):
        tail = jnp.concatenate([t[src] for t in tails], axis=0).astype(jnp.float32)
        grow = jnp.exp2(tail[SCALE_ROW - TAIL : SCALE_ROW - TAIL + 1] * 0.0625) / LEVELS
        grow_ref[src * 8 : src * 8 + 8, :] = jnp.broadcast_to(grow, (8, 128))
        tail_ref[src * 80 : (src + 1) * 80, :] = tail * grow


def turn(rows_of, slabs, tail_ref, grow_ref, turn_ref):
    lane = lax.broadcasted_iota(jnp.int32, (8, 128), 1)
    line = lax.broadcasted_iota(jnp.int32, (8, 128), 0)
    for src in range(16):
        grow = grow_ref[src * 8 : src * 8 + 8, :]
        halves = []
        for which in range(2):
            both = rows_of(src, which).astype(jnp.float32)
            above = tail_ref[pl.ds((src + 1) % 16 * 80 + slabs[which], 1), :]
            below = tail_ref[pl.ds((src + 15) % 16 * 80 + 40 + slabs[which], 1), :]
            upper = both[0:8] * grow + jnp.where(line == 0, below, 0.0)
            lower = both[8:16] * grow + jnp.where(line == 7, above, 0.0)
            halves.append((upper, lower))
        for half in range(2):
            da, db = halves[0][half], halves[1][half]
            begin = src * 32 + half * 16
            turn_ref[pl.ds(begin, 8, stride=2), :] = jnp.where(lane & 32 == 0, da, pltpu.roll(db, 32, 1))
            turn_ref[pl.ds(begin + 1, 8, stride=2), :] = jnp.where(lane & 32 == 0, pltpu.roll(da, 96, 1), db)
    blocks = []
    for c in range(4):
        block = turn_ref[c * 128 : (c + 1) * 128, :].T.reshape(2, 2, 4, 8, 128)
        blocks.append([jnp.concatenate([block[0, which], block[1, which]], axis=0) for which in range(2)])
    return blocks


def edge_kernel(low_ref, high_ref, *refs):
    tails, (down_ref, up_ref), scratch = refs[:5], refs[5:7], refs[7:]
    take_tails(tails, *scratch[:2])
    blocks = turn(lambda src, which: (low_ref, high_ref)[which][src], (0, VOUT - 1), *scratch[:2], scratch[2].at[0])
    for c, block in enumerate(blocks):
        down_ref[:, :, c * 128 : (c + 1) * 128] = block[0][:, 6:8]
        up_ref[:, :, c * 128 : (c + 1) * 128] = block[1][:, 0:2]


def assemble(x_ref, first, out_ref, scratch):
    tail_ref, grow_ref, turn_refs = scratch
    for pair in range(2):
        rows_of = lambda src, which: x_ref[src, (2 * pair + which) * 16 : (2 * pair + which + 1) * 16, :]
        slabs = (first + 2 * pair, first + 2 * pair + 1)
        blocks = turn(rows_of, slabs, tail_ref, grow_ref, turn_refs.at[pair])
        for c, block in enumerate(blocks):
            for which in range(2):
                begin = pair * 16 + which * 8
                out_ref[:, begin : begin + 8, c * 128 : (c + 1) * 128] = block[which]


def inner_kernel(x_ref, *refs):
    tails, out_ref, scratch = refs[:5], refs[5], refs[6:]
    step = pl.program_id(0)

    @pl.when(step == 0)
    def _():
        take_tails(tails, *scratch[:2])

    assemble(x_ref, 4 * step + 5, out_ref, scratch)


def outer_kernel(x_ref, *refs):
    tails, (below_ref, above_ref, _, out_ref), scratch = refs[:5], refs[5:9], refs[9:]
    step = pl.program_id(0)

    @pl.when(step == 0)
    def _():
        take_tails(tails, *scratch[:2])

    assemble(x_ref, 28 * step + 1, out_ref, scratch)

    @pl.when(step == 0)
    def _():
        out_ref[:, 0:2, :] += below_ref[...]

    @pl.when(step == 1)
    def _():
        out_ref[:, 30:32, :] += above_ref[...]


def from_behind(block, axis, distance):
    devices = range(lax.axis_size(axis))
    route = [((i - distance) % len(devices), i) for i in devices]
    return lax.ppermute(block, axis, route)


def on_device(charges, weight_tiles, block_shape, block_box, live_blocks):
    nblk, atoms = charges.shape
    shapes_n, _, cells = weight_tiles.shape
    wflat = weight_tiles.reshape(shapes_n * atoms, cells)
    rows = (nblk // 128, 128)
    vmem = pl.BlockSpec(memory_space=pltpu.VMEM)
    smem = pl.BlockSpec(memory_space=pltpu.SMEM)
    hbm = pl.BlockSpec(memory_space=pl.ANY)
    sent = pl.pallas_call(
        spread_kernel,
        out_shape=jax.ShapeDtypeStruct((KZ, SENT, 128), WIRE),
        in_specs=[smem] + [vmem] * 3 + [hbm] * 2,
        out_specs=vmem,
        scratch_shapes=[
            pltpu.VMEM((GROWS + SPARE, 128), jnp.float32),
            pltpu.VMEM((shapes_n * atoms, cells), jnp.bfloat16),
            pltpu.VMEM((1024, 384), jnp.bfloat16),
            pltpu.VMEM((GROUP, shapes_n * atoms), jnp.bfloat16),
            pltpu.VMEM((GROUP, 1024), jnp.bfloat16),
            pltpu.VMEM((GROUP, 1024), jnp.bfloat16),
            pltpu.VMEM((GROUP, 128), jnp.float32),
            pltpu.VMEM((GROUP, 128), jnp.float32),
            pltpu.VMEM((GROUP * 4, 128), jnp.float32),
            pltpu.VMEM((GROUP * 4, 128), jnp.float32),
            pltpu.VMEM((SENT, 128), jnp.float32),
            pltpu.VMEM(rows, jnp.int32),
            pltpu.VMEM(rows, jnp.int32),
            pltpu.VMEM(rows, jnp.int32),
            pltpu.VMEM(rows, jnp.float32),
            pltpu.SMEM(rows, jnp.int32),
            pltpu.SMEM(rows, jnp.int32),
            pltpu.SMEM(rows, jnp.int32),
            pltpu.SemaphoreType.DMA((5,)),
        ],
        compiler_params=pltpu.CompilerParams(vmem_limit_bytes=56 * 1024 * 1024),
        name="spread",
    )(
        live_blocks,
        charges,
        block_shape.reshape(rows),
        block_box.reshape(rows),
        wflat,
        jnp.asarray(restriction(), jnp.bfloat16),
    )
    got = lax.all_to_all(sent, "bx", split_axis=0, concat_axis=0, tiled=True)
    piece = lambda i: pl.BlockSpec((KZ, 16, 128), lambda p: (0, i, 0))
    tails = [piece(TAIL // 16 + i) for i in range(5)]
    small = pl.BlockSpec((8, 2, 512), lambda p: (0, 0, 0))
    full = jax.ShapeDtypeStruct((8, 256, 512), jnp.float32)
    scratch = [
        pltpu.VMEM((16 * 80, 128), jnp.float32),
        pltpu.VMEM((128, 128), jnp.float32),
        pltpu.VMEM((2, 512, 128), jnp.float32),
    ]
    params = pltpu.CompilerParams(vmem_limit_bytes=40 * 1024 * 1024)
    down, up = pl.pallas_call(
        edge_kernel,
        out_shape=(jax.ShapeDtypeStruct((8, 2, 512), jnp.float32),) * 2,
        grid=(1,),
        in_specs=[piece(VOUT - 2), piece(VOUT - 1)] + tails,
        out_specs=(small, small),
        scratch_shapes=scratch,
        compiler_params=params,
        name="edge",
    )(*[got] * 7)
    below = from_behind(up, "by", 1)
    above = from_behind(down, "by", -1)
    inner = pl.pallas_call(
        inner_kernel,
        out_shape=full,
        grid=(6,),
        in_specs=[pl.BlockSpec((KZ, 64, 128), lambda p: (0, p + 1, 0))] + tails,
        out_specs=pl.BlockSpec((8, 32, 512), lambda p: (0, p + 1, 0)),
        scratch_shapes=scratch,
        compiler_params=params,
        name="inner",
    )(*[got] * 6)
    return pl.pallas_call(
        outer_kernel,
        out_shape=full,
        grid=(2,),
        in_specs=[pl.BlockSpec((KZ, 64, 128), lambda p: (0, 7 * p, 0))]
        + tails
        + [small, small, pl.BlockSpec(memory_space=pl.ANY)],
        out_specs=pl.BlockSpec((8, 32, 512), lambda p: (0, 7 * p, 0)),
        scratch_shapes=scratch,
        input_output_aliases={8: 0},
        compiler_params=params,
        name="outer",
    )(*[got] * 6, below, above, inner)


def solution(mesh):
    return jax.shard_map(
        on_device,
        mesh=mesh,
        in_specs=(P(("bx", "by"), None), P(), P(("bx", "by")), P(("bx", "by")), P(("bx", "by"))),
        out_specs=P("bx", "by", None),
        check_vma=False,
    )
```

```python
import jax
import jax.numpy as jnp
import numpy as np
from jax import lax
from jax.experimental import pallas as pl
from jax.experimental.pallas import tpu as pltpu
from jax.sharding import PartitionSpec as P

NZ = 128
GROUP = 256
BATCH = 16
KZ = 16
UROWS = 24
VSLOTS = 34
FRONT = VSLOTS * UROWS
PLANE = UROWS * VSLOTS
GROWS = FRONT + 4 * KZ * PLANE
SPARE = -GROWS % 256 + 256
DUMP = GROWS + SPARE - 8
EDGE = 512
TAIL = EDGE + 16
SENT = TAIL + 80
WIRE = jnp.int16
LEVELS = 32700.0
UNROLL = 11
SCALE_ROW = TAIL + 33


def restriction():
    coef = [1.0, 4.0, 6.0, 4.0, 1.0]
    table = np.zeros((512, 384), np.float32)
    for p in range(8):
        for mm in range(6):
            tap = p + 4 - 2 * mm
            if not 0 <= tap < 5:
                continue
            for q in range(8):
                for r in range(8):
                    z, y = (r - 2) % 8, (q - 2) % 8
                    lane = z // 4 * 64 + mm % 2 * 32 + z % 4 * 8 + y
                    table[(p * 8 + q) * 8 + r, mm // 2 * 128 + lane] = coef[tap] / 8.0
    return np.concatenate([table, table], axis=0)


def place_blocks(shape_ref, box_ref, live, base_ref, fast_ref, flag_ref, code_ref):
    lane = lax.broadcasted_iota(jnp.int32, base_ref.shape, 1)
    slot = lax.broadcasted_iota(jnp.int32, base_ref.shape, 0) * 128 + lane
    box = box_ref[...]
    u = box >> 11
    v = (box >> 5) & 63
    w = box & 31
    kind = (w & 1) * 2 + (v & 1)
    base = FRONT + (kind * KZ + (w >> 1)) * PLANE + (v >> 1) * UROWS + 7 + u
    late = jnp.zeros(base.shape, jnp.int32)
    for d in range(1, BATCH):
        near = jnp.abs(base - pltpu.roll(base, d, 1)) < 3
        late = jnp.where(near & ((lane & (BATCH - 1)) >= d), 1, late)
    base_ref[...] = base
    fast_ref[...] = jnp.where(late == 1, DUMP, base)
    for d in (1, 2, 4, 8):
        late = late | pltpu.roll(late, 128 - d, 1)
    flag_ref[...] = late
    code = jnp.where(slot < live, shape_ref[...], 32) * 4 + kind
    code_ref[...] = code.astype(jnp.float32)


def spread_kernel(live_ref, q_ref, shape_ref, box_ref, w_any, r_any, out_any, *scratch):
    grid_ref, w_ref, r_ref, pick_ref, half_a, half_b, kind_a, kind_b, tile_a, tile_b, plane_ref = scratch[:11]
    base_v, fast_v, flag_v, code_ref, base_ref, fast_ref, flag_ref, out_ref, sems, out_sems = scratch[11:]
    shapes_n = w_ref.shape[0] // 128
    copies = [pltpu.make_async_copy(w_any, w_ref, sems.at[0]), pltpu.make_async_copy(r_any, r_ref, sems.at[1])]
    for copy in copies:
        copy.start()
    place_blocks(shape_ref, box_ref, live_ref[0], base_v, fast_v, flag_v, code_ref)
    for i, (here, there) in enumerate(((base_v, base_ref), (fast_v, fast_ref), (flag_v, flag_ref))):
        copies.append(pltpu.make_async_copy(here, there, sems.at[2 + i]))
        copies[-1].start()
    for ref in (half_b, kind_b, tile_a):
        ref[...] = jnp.zeros(ref.shape, ref.dtype)

    def clear(step, carry):
        grid_ref[pl.ds(pl.multiple_of(step * 256, 256), 256), :] = jnp.zeros((256, 128), jnp.float32)
        return carry

    lax.fori_loop(0, (GROWS + SPARE) // 256, clear, 0)
    for copy in copies:
        copy.wait()

    def product(step, half_ref, kind_ref):
        begin = pl.multiple_of(step * GROUP, GROUP)
        qg = q_ref[pl.ds(begin, GROUP), :]
        codes = [code_ref[pl.ds(step * (GROUP // 128) + h, 1), :] for h in range(GROUP // 128)]
        code = jnp.concatenate([jnp.broadcast_to(c, (128, 128)).T for c in codes], axis=0)
        whole = jnp.floor(code * 0.25)
        sg = whole.astype(jnp.bfloat16)
        kind_ref[...] = code - 4.0 * whole
        part = jnp.zeros((GROUP, 512), jnp.float32)
        for s in range(0, shapes_n, 2):
            pick = jnp.concatenate([jnp.where(sg == s + i, qg, jnp.zeros_like(qg)) for i in range(2)], axis=1)
            part += jnp.dot(pick, w_ref[s * 128 : (s + 2) * 128, :], preferred_element_type=jnp.float32)
        high = part.astype(jnp.bfloat16)
        half_ref[:, :512] = high
        half_ref[:, 512:] = (part - high.astype(jnp.float32)).astype(jnp.bfloat16)

    def arrange(half_ref, kind_ref, tile_ref):
        cells = jnp.dot(half_ref[...], r_ref[...], preferred_element_type=jnp.float32)
        kind = kind_ref[...]
        z_odd = kind >= 2.0
        y_odd = (kind == 1.0) | (kind == 3.0)
        y_upper = (lax.broadcasted_iota(jnp.int32, kind.shape, 1) & 4) != 0
        for du in range(3):
            rows = cells[:, du * 128 : (du + 1) * 128]
            rows = jnp.where(z_odd, pltpu.roll(rows, 64, 1), rows)
            crossed = jnp.where(y_upper, pltpu.roll(rows, 4, 1), pltpu.roll(rows, 124, 1))
            tile_ref[pl.ds(du, GROUP, stride=4), :] = jnp.where(y_odd, crossed, rows)

    def at(ref, step, i):
        return ref[step * (GROUP // 128) + i // 128, i % 128]

    def deposit(step, tile_ref):
        for batch in range(GROUP // BATCH):
            slots = [batch * BATCH + j for j in range(BATCH)]
            rows = [at(fast_ref, step, i) for i in slots]
            sums = [grid_ref[pl.ds(r, 3), :] + tile_ref[4 * i : 4 * i + 3, :] for r, i in zip(rows, slots)]
            for r, value in zip(rows, sums):
                grid_ref[pl.ds(r, 3), :] = value

    def deposit_rest(step, tile_ref):
        flag = at(flag_ref, step, 0)
        for batch in range(1, GROUP // BATCH):
            flag = flag | at(flag_ref, step, batch * BATCH)

        @pl.when(flag != 0)
        def _():
            def one_batch(batch, carry):
                row = step * (GROUP // 128) + batch // (128 // BATCH)
                head = batch % (128 // BATCH) * BATCH

                @pl.when(flag_ref[row, head] != 0)
                def _():
                    def one_block(j, inner):
                        spot = base_ref[row, head + j]

                        @pl.when(fast_ref[row, head + j] != spot)
                        def _():
                            grid_ref[pl.ds(spot, 3), :] += tile_ref[pl.ds((batch * BATCH + j) * 4, 3), :]

                        return inner

                    lax.fori_loop(0, BATCH, one_block, 0)

                return carry

            lax.fori_loop(0, GROUP // BATCH, one_batch, 0)

    def two_groups(pair, carry):
        step = 2 * pair
        arrange(half_b, kind_b, tile_b)
        product(step, half_a, kind_a)
        deposit(jnp.maximum(step - 2, 0), tile_a)
        arrange(half_a, kind_a, tile_a)
        product(step + 1, half_b, kind_b)
        deposit(jnp.maximum(step - 1, 0), tile_b)

        @pl.when(pair > 0)
        def _():
            deposit_rest(step - 1, tile_b)

        deposit_rest(step, tile_a)
        return carry

    pairs = (live_ref[0] + 2 * GROUP - 1) // (2 * GROUP)
    lax.fori_loop(0, pairs, two_groups, 0)
    arrange(half_b, kind_b, tile_b)
    deposit(2 * pairs - 2, tile_a)
    deposit(2 * pairs - 1, tile_b)
    deposit_rest(2 * pairs - 1, tile_b)

    def out_copy(k):
        return pltpu.make_async_copy(out_ref.at[k], out_any.at[k], out_sems.at[k])

    def two_planes(pair, carry):
        combine(2 * pair, grid_ref, plane_ref)
        for i in range(2):
            encode(plane_ref.at[i], out_ref.at[2 * pair + i])
            out_copy(2 * pair + i).start()
        return carry

    lax.fori_loop(0, KZ // 2, two_planes, 0)
    for k in range(KZ):
        out_copy(k).wait()


def combine(k, grid_ref, plane_ref):
    lane = lax.broadcasted_iota(jnp.int32, (8, 128), 1)
    z = ((lane >> 6) << 2) + ((lane >> 3) & 3)
    z_kept = z < 6
    z_past = z < 2
    y_kept = (lane & 7) < 6
    y_past = (lane & 7) < 2
    last_k = lax.rem(k + KZ - 1, KZ)
    third_k = lax.rem(k + 2, KZ)

    def slabs(odd, row):
        def at(copy, plane):
            return grid_ref[pl.ds(pl.multiple_of(FRONT + (copy * KZ + plane) * PLANE + row, 8), 8), :]

        even = [at(odd, p) for p in (k, k + 1, third_k)]
        odd = [at(2 + odd, p) for p in (last_k, k, k + 1)]
        return [jnp.where(z_kept, even[i], even[i + 1]) + jnp.where(z_past, odd[i], odd[i + 1]) for i in range(2)]

    def put_ends(i, below, above, value):
        plane_ref[i, pl.ds(TAIL + below, 1), :] = value[7:8]
        plane_ref[i, pl.ds(TAIL + 40 + above, 1), :] = value[0:1]

    def one_slab(v, carry):
        evens, odds = carry
        place = jnp.where(v == 0, 32, v - 1)
        above = jnp.where(v < 2, 33 - v, v - 2)
        new_evens, new_odds = [], []
        for part in range(3):
            row = v * UROWS + 8 * part
            even, odd = slabs(0, row), slabs(1, row - UROWS)
            for i in range(2):
                value = jnp.where(y_kept, evens[part][i], even[i]) + jnp.where(y_past, odds[part][i], odd[i])
                if part == 0:
                    put_ends(i, place, above, value)
                else:
                    plane_ref[i, pl.ds(pl.multiple_of(place * 16 + 8 * part - 8, 8), 8), :] = value
            new_evens.append(even)
            new_odds.append(odd)
        return new_evens, new_odds

    zero = jnp.zeros((8, 128), jnp.float32)
    start = [[zero] * 2] * 3
    evens, odds = lax.fori_loop(0, 33, one_slab, (start, start), unroll=UNROLL)
    odd = slabs(1, 32 * UROWS)
    for i in range(2):
        for part in (1, 2):
            begin = EDGE + 8 * part - 8
            plane_ref[i, begin : begin + 8, :] += jnp.where(y_past, odds[part][i], 0.0)
        value = jnp.where(y_kept, evens[0][i], 0.0) + jnp.where(y_past, odds[0][i], odd[i])
        plane_ref[i, TAIL + 32 : TAIL + 33, :] += value[7:8]
        plane_ref[i, TAIL + 71 : TAIL + 72, :] = value[0:1]
        plane_ref[i, TAIL + 72 : TAIL + 73, :] += jnp.where(y_past, odd[i], 0.0)[0:1]


def encode(plane_ref, out_ref):
    line = lax.broadcasted_iota(jnp.int32, (8, 128), 0)
    top = jnp.max(jnp.abs(plane_ref[: TAIL + 33, :]), axis=0, keepdims=True)
    top = jnp.maximum(top, jnp.max(jnp.abs(plane_ref[TAIL + 40 : TAIL + 73, :]), axis=0, keepdims=True))
    power = jnp.ceil(jnp.log2(jnp.maximum(top, 1e-37)) * 16.0 + 0.01)
    shrink = jnp.exp2(power * -0.0625)
    whole = jnp.round(plane_ref[...] * shrink * LEVELS)
    out_ref[...] = whole.astype(jnp.int32).astype(out_ref.dtype)
    begin = SCALE_ROW // 16 * 16
    marked = jnp.round(plane_ref[begin : begin + 8, :] * shrink * LEVELS)
    marked = jnp.where(line == SCALE_ROW - begin, power, marked)
    rest = jnp.round(plane_ref[begin + 8 : begin + 16, :] * shrink * LEVELS)
    out_ref[begin : begin + 16, :] = jnp.concatenate([marked, rest], axis=0).astype(jnp.int32).astype(out_ref.dtype)


def take_tails(tails, tail_ref, grow_ref):
    for src in range(16):
        tail = jnp.concatenate([t[src] for t in tails], axis=0).astype(jnp.float32)
        grow = jnp.exp2(tail[SCALE_ROW - TAIL : SCALE_ROW - TAIL + 1] * 0.0625) / LEVELS
        grow_ref[src * 8 : src * 8 + 8, :] = jnp.broadcast_to(grow, (8, 128))
        tail_ref[src * 80 : (src + 1) * 80, :] = tail * grow


def turn(rows_of, slabs, tail_ref, grow_ref, turn_ref):
    lane = lax.broadcasted_iota(jnp.int32, (8, 128), 1)
    line = lax.broadcasted_iota(jnp.int32, (8, 128), 0)
    for src in range(16):
        grow = grow_ref[src * 8 : src * 8 + 8, :]
        halves = []
        for which in range(len(slabs)):
            both = rows_of(src, which).astype(jnp.float32)
            above = tail_ref[pl.ds((src + 1) % 16 * 80 + slabs[which], 1), :]
            below = tail_ref[pl.ds((src + 15) % 16 * 80 + 40 + slabs[which], 1), :]
            upper = both[0:8] * grow + jnp.where(line == 0, below, 0.0)
            lower = both[8:16] * grow + jnp.where(line == 7, above, 0.0)
            halves.append((upper, lower))
        if len(slabs) == 1:
            halves.append((jnp.zeros((8, 128), jnp.float32),) * 2)
        for half in range(2):
            da, db = halves[0][half], halves[1][half]
            begin = src * 32 + half * 16
            turn_ref[pl.ds(begin, 8, stride=2), :] = jnp.where(lane & 32 == 0, da, pltpu.roll(db, 32, 1))
            turn_ref[pl.ds(begin + 1, 8, stride=2), :] = jnp.where(lane & 32 == 0, pltpu.roll(da, 96, 1), db)
    blocks = []
    for c in range(4):
        block = turn_ref[c * 128 : (c + 1) * 128, :].T.reshape(2, 2, 4, 8, 128)
        blocks.append([jnp.concatenate([block[0, which], block[1, which]], axis=0) for which in range(2)])
    return blocks


def edge_kernel(x_ref, *refs):
    tails, (down_ref, up_ref), scratch = refs[:5], refs[5:7], refs[7:]
    take_tails(tails, *scratch[:2])
    blocks = turn(lambda src, which: x_ref[src], (32,), *scratch[:2], scratch[2].at[0])
    for c, block in enumerate(blocks):
        down_ref[:, :, c * 128 : (c + 1) * 128] = block[0][:, 6:8]
        up_ref[:, :, c * 128 : (c + 1) * 128] = block[0][:, 0:2]


def assemble(x_ref, first, out_ref, scratch):
    tail_ref, grow_ref, turn_refs = scratch
    for pair in range(2):
        rows_of = lambda src, which: x_ref[src, (2 * pair + which) * 16 : (2 * pair + which + 1) * 16, :]
        slabs = (first + 2 * pair, first + 2 * pair + 1)
        blocks = turn(rows_of, slabs, tail_ref, grow_ref, turn_refs.at[pair])
        for c, block in enumerate(blocks):
            for which in range(2):
                begin = pair * 16 + which * 8
                out_ref[:, begin : begin + 8, c * 128 : (c + 1) * 128] = block[which]


def inner_kernel(x_ref, *refs):
    tails, out_ref, scratch = refs[:5], refs[5], refs[6:]
    step = pl.program_id(0)

    @pl.when(step == 0)
    def _():
        take_tails(tails, *scratch[:2])

    assemble(x_ref, 4 * step + 4, out_ref, scratch)


def outer_kernel(x_ref, *refs):
    tails, (below_ref, above_ref, _, out_ref), scratch = refs[:5], refs[5:9], refs[9:]
    step = pl.program_id(0)

    @pl.when(step == 0)
    def _():
        take_tails(tails, *scratch[:2])

    assemble(x_ref, 28 * step, out_ref, scratch)

    @pl.when(step == 0)
    def _():
        out_ref[:, 0:2, :] += below_ref[...]

    @pl.when(step == 1)
    def _():
        out_ref[:, 30:32, :] += above_ref[...]


def from_behind(block, axis, distance):
    devices = range(lax.axis_size(axis))
    route = [((i - distance) % len(devices), i) for i in devices]
    return lax.ppermute(block, axis, route)


def on_device(charges, weight_tiles, block_shape, block_box, live_blocks):
    nblk, atoms = charges.shape
    shapes_n, _, cells = weight_tiles.shape
    wflat = weight_tiles.reshape(shapes_n * atoms, cells)
    rows = (nblk // 128, 128)
    vmem = pl.BlockSpec(memory_space=pltpu.VMEM)
    smem = pl.BlockSpec(memory_space=pltpu.SMEM)
    hbm = pl.BlockSpec(memory_space=pl.ANY)
    sent = pl.pallas_call(
        spread_kernel,
        out_shape=jax.ShapeDtypeStruct((KZ, SENT, 128), WIRE),
        in_specs=[smem] + [vmem] * 3 + [hbm] * 2,
        out_specs=hbm,
        scratch_shapes=[
            pltpu.VMEM((GROWS + SPARE, 128), jnp.float32),
            pltpu.VMEM((shapes_n * atoms, cells), jnp.bfloat16),
            pltpu.VMEM((1024, 384), jnp.bfloat16),
            pltpu.VMEM((GROUP, shapes_n * atoms), jnp.bfloat16),
            pltpu.VMEM((GROUP, 1024), jnp.bfloat16),
            pltpu.VMEM((GROUP, 1024), jnp.bfloat16),
            pltpu.VMEM((GROUP, 128), jnp.float32),
            pltpu.VMEM((GROUP, 128), jnp.float32),
            pltpu.VMEM((GROUP * 4, 128), jnp.float32),
            pltpu.VMEM((GROUP * 4, 128), jnp.float32),
            pltpu.VMEM((2, SENT, 128), jnp.float32),
            pltpu.VMEM(rows, jnp.int32),
            pltpu.VMEM(rows, jnp.int32),
            pltpu.VMEM(rows, jnp.int32),
            pltpu.VMEM(rows, jnp.float32),
            pltpu.SMEM(rows, jnp.int32),
            pltpu.SMEM(rows, jnp.int32),
            pltpu.SMEM(rows, jnp.int32),
            pltpu.VMEM((KZ, SENT, 128), WIRE),
            pltpu.SemaphoreType.DMA((5,)),
            pltpu.SemaphoreType.DMA((KZ,)),
        ],
        compiler_params=pltpu.CompilerParams(vmem_limit_bytes=56 * 1024 * 1024),
        name="spread",
    )(
        live_blocks,
        charges,
        block_shape.reshape(rows),
        block_box.reshape(rows),
        wflat,
        jnp.asarray(restriction(), jnp.bfloat16),
    )
    got = lax.all_to_all(sent, "bx", split_axis=0, concat_axis=0, tiled=True)
    piece = lambda i: pl.BlockSpec((KZ, 16, 128), lambda p: (0, i, 0))
    tails = [piece(TAIL // 16 + i) for i in range(5)]
    small = pl.BlockSpec((8, 2, 512), lambda p: (0, 0, 0))
    full = jax.ShapeDtypeStruct((8, 256, 512), jnp.float32)
    scratch = [
        pltpu.VMEM((16 * 80, 128), jnp.float32),
        pltpu.VMEM((128, 128), jnp.float32),
        pltpu.VMEM((2, 512, 128), jnp.float32),
    ]
    params = pltpu.CompilerParams(vmem_limit_bytes=40 * 1024 * 1024)
    down, up = pl.pallas_call(
        edge_kernel,
        out_shape=(jax.ShapeDtypeStruct((8, 2, 512), jnp.float32),) * 2,
        grid=(1,),
        in_specs=[piece(EDGE // 16)] + tails,
        out_specs=(small, small),
        scratch_shapes=scratch,
        compiler_params=params,
        name="edge",
    )(*[got] * 6)
    below = from_behind(up, "by", 1)
    above = from_behind(down, "by", -1)
    inner = pl.pallas_call(
        inner_kernel,
        out_shape=full,
        grid=(6,),
        in_specs=[pl.BlockSpec((KZ, 64, 128), lambda p: (0, p + 1, 0))] + tails,
        out_specs=pl.BlockSpec((8, 32, 512), lambda p: (0, p + 1, 0)),
        scratch_shapes=scratch,
        compiler_params=params,
        name="inner",
    )(*[got] * 6)
    return pl.pallas_call(
        outer_kernel,
        out_shape=full,
        grid=(2,),
        in_specs=[pl.BlockSpec((KZ, 64, 128), lambda p: (0, 7 * p, 0))]
        + tails
        + [small, small, pl.BlockSpec(memory_space=pl.ANY)],
        out_specs=pl.BlockSpec((8, 32, 512), lambda p: (0, 7 * p, 0)),
        scratch_shapes=scratch,
        input_output_aliases={8: 0},
        compiler_params=params,
        name="outer",
    )(*[got] * 6, below, above, inner)


def solution(mesh):
    return jax.shard_map(
        on_device,
        mesh=mesh,
        in_specs=(P(("bx", "by"), None), P(), P(("bx", "by")), P(("bx", "by")), P(("bx", "by"))),
        out_specs=P("bx", "by", None),
        check_vma=False,
    )
```

```python
import functools

import jax
import jax.numpy as jnp
import numpy as np
from jax import lax
from jax.experimental import pallas as pl
from jax.experimental.pallas import tpu as pltpu
from jax.sharding import PartitionSpec as P

NZ = 128
GROUP = 256
BATCH = 16
KZ = 16
UROWS = 24
VSLOTS = 34
FRONT = VSLOTS * UROWS
PLANE = UROWS * VSLOTS
GROWS = FRONT + 4 * KZ * PLANE
SPARE = -GROWS % 256 + 256
DUMP = GROWS + SPARE - 8
EDGE = 512
TAIL = EDGE + 16
SENT = TAIL + 80
WIRE = jnp.int16
LEVELS = 32700.0
UNROLL = 11
SCALE_ROW = TAIL + 33


def restriction():
    coef = [1.0, 4.0, 6.0, 4.0, 1.0]
    table = np.zeros((512, 384), np.float32)
    for p in range(8):
        for mm in range(6):
            tap = p + 4 - 2 * mm
            if not 0 <= tap < 5:
                continue
            for q in range(8):
                for r in range(8):
                    z, y = (r - 2) % 8, (q - 2) % 8
                    lane = z // 4 * 64 + mm % 2 * 32 + z % 4 * 8 + y
                    table[(p * 8 + q) * 8 + r, mm // 2 * 128 + lane] = coef[tap] / 8.0
    return np.concatenate([table, table], axis=0)


def place_blocks(shape_ref, box_ref, live, base_ref, fast_ref, first_ref, many_ref, code_ref):
    lane = lax.broadcasted_iota(jnp.int32, base_ref.shape, 1)
    slot = lax.broadcasted_iota(jnp.int32, base_ref.shape, 0) * 128 + lane
    box = box_ref[...]
    u = box >> 11
    v = (box >> 5) & 63
    w = box & 31
    kind = (w & 1) * 2 + (v & 1)
    base = FRONT + (kind * KZ + (w >> 1)) * PLANE + (v >> 1) * UROWS + 7 + u
    late = jnp.zeros(base.shape, jnp.int32)
    for d in range(1, BATCH):
        near = jnp.abs(base - pltpu.roll(base, d, 1)) < 3
        late = jnp.where(near & ((lane & (BATCH - 1)) >= d), 1, late)
    base_ref[...] = base
    fast_ref[...] = jnp.where(late == 1, DUMP, base)
    first = jnp.where(late == 1, lane & (BATCH - 1), BATCH)
    for d in (1, 2, 4, 8):
        first = jnp.minimum(first, pltpu.roll(first, 128 - d, 1))
        late = late + pltpu.roll(late, 128 - d, 1)
    first_ref[...] = first
    many_ref[...] = jnp.where(late > 1, 1, 0)
    code = jnp.where(slot < live, shape_ref[...], 32) * 4 + kind
    code_ref[...] = code.astype(jnp.float32)


def spread_kernel(live_ref, q_ref, shape_ref, box_ref, w_any, r_any, out_any, *scratch):
    grid_ref, w_ref, r_ref, pick_ref, half_a, half_b, kind_a, kind_b, tile_a, tile_b, plane_ref = scratch[:11]
    base_v, fast_v, first_v, many_v, code_ref, base_ref, fast_ref, first_ref, many_ref = scratch[11:20]
    out_ref, sems, out_sems = scratch[20:]
    shapes_n = w_ref.shape[0] // 128
    copies = [pltpu.make_async_copy(w_any, w_ref, sems.at[0]), pltpu.make_async_copy(r_any, r_ref, sems.at[1])]
    for copy in copies:
        copy.start()
    place_blocks(shape_ref, box_ref, live_ref[0], base_v, fast_v, first_v, many_v, code_ref)
    places = ((base_v, base_ref), (fast_v, fast_ref), (first_v, first_ref), (many_v, many_ref))
    for i, (here, there) in enumerate(places):
        copies.append(pltpu.make_async_copy(here, there, sems.at[2 + i]))
        copies[-1].start()
    for ref in (half_b, kind_b, tile_a):
        ref[...] = jnp.zeros(ref.shape, ref.dtype)

    def clear(step, carry):
        grid_ref[pl.ds(pl.multiple_of(step * 256, 256), 256), :] = jnp.zeros((256, 128), jnp.float32)
        return carry

    lax.fori_loop(0, (GROWS + SPARE) // 256, clear, 0)
    for copy in copies:
        copy.wait()

    def product(step, half_ref, kind_ref):
        begin = pl.multiple_of(step * GROUP, GROUP)
        qg = q_ref[pl.ds(begin, GROUP), :]
        codes = [code_ref[pl.ds(step * (GROUP // 128) + h, 1), :] for h in range(GROUP // 128)]
        code = jnp.concatenate([jnp.broadcast_to(c, (128, 128)).T for c in codes], axis=0)
        whole = jnp.floor(code * 0.25)
        sg = whole.astype(jnp.bfloat16)
        kind_ref[...] = code - 4.0 * whole
        part = jnp.zeros((GROUP, 512), jnp.float32)
        for s in range(0, shapes_n, 2):
            pick = jnp.concatenate([jnp.where(sg == s + i, qg, jnp.zeros_like(qg)) for i in range(2)], axis=1)
            part += jnp.dot(pick, w_ref[s * 128 : (s + 2) * 128, :], preferred_element_type=jnp.float32)
        high = part.astype(jnp.bfloat16)
        half_ref[:, :512] = high
        half_ref[:, 512:] = (part - high.astype(jnp.float32)).astype(jnp.bfloat16)

    def arrange(half_ref, kind_ref, tile_ref):
        cells = jnp.dot(half_ref[...], r_ref[...], preferred_element_type=jnp.float32)
        kind = kind_ref[...]
        z_odd = kind >= 2.0
        y_odd = (kind == 1.0) | (kind == 3.0)
        y_upper = (lax.broadcasted_iota(jnp.int32, kind.shape, 1) & 4) != 0
        for du in range(3):
            rows = cells[:, du * 128 : (du + 1) * 128]
            rows = jnp.where(z_odd, pltpu.roll(rows, 64, 1), rows)
            crossed = jnp.where(y_upper, pltpu.roll(rows, 4, 1), pltpu.roll(rows, 124, 1))
            tile_ref[pl.ds(du, GROUP, stride=4), :] = jnp.where(y_odd, crossed, rows)

    def at(ref, step, i):
        return ref[step * (GROUP // 128) + i // 128, i % 128]

    def deposit(step, tile_ref):
        for batch in range(GROUP // BATCH):
            slots = [batch * BATCH + j for j in range(BATCH)]
            rows = [at(fast_ref, step, i) for i in slots]
            sums = [grid_ref[pl.ds(r, 3), :] + tile_ref[4 * i : 4 * i + 3, :] for r, i in zip(rows, slots)]
            for r, value in zip(rows, sums):
                grid_ref[pl.ds(r, 3), :] = value

    def deposit_rest(step, tile_ref):
        heads = range(0, GROUP, BATCH)
        firsts = [at(first_ref, step, i) for i in heads]

        @pl.when(functools.reduce(jnp.minimum, firsts) < BATCH)
        def _():
            for i, first in zip(heads, firsts):
                held = jnp.minimum(first, BATCH - 1)
                spot = base_ref[step * (GROUP // 128) + i // 128, i % 128 + held]
                spot = jnp.where(first < BATCH, spot, DUMP)
                grid_ref[pl.ds(spot, 3), :] += tile_ref[pl.ds((i + held) * 4, 3), :]

        @pl.when(functools.reduce(jnp.maximum, [at(many_ref, step, i) for i in heads]) > 0)
        def _():
            def one_batch(batch, carry):
                row = step * (GROUP // 128) + batch // (128 // BATCH)
                head = batch % (128 // BATCH) * BATCH

                @pl.when(many_ref[row, head] != 0)
                def _():
                    def one_block(j, inner):
                        spot = base_ref[row, head + j]

                        @pl.when((fast_ref[row, head + j] != spot) & (first_ref[row, head] != j))
                        def _():
                            grid_ref[pl.ds(spot, 3), :] += tile_ref[pl.ds((batch * BATCH + j) * 4, 3), :]

                        return inner

                    lax.fori_loop(0, BATCH, one_block, 0)

                return carry

            lax.fori_loop(0, GROUP // BATCH, one_batch, 0)

    def two_groups(pair, carry):
        step = 2 * pair
        arrange(half_b, kind_b, tile_b)
        product(step, half_a, kind_a)
        deposit(jnp.maximum(step - 2, 0), tile_a)
        arrange(half_a, kind_a, tile_a)
        product(step + 1, half_b, kind_b)
        deposit(jnp.maximum(step - 1, 0), tile_b)

        @pl.when(pair > 0)
        def _():
            deposit_rest(step - 1, tile_b)

        deposit_rest(step, tile_a)
        return carry

    pairs = (live_ref[0] + 2 * GROUP - 1) // (2 * GROUP)
    lax.fori_loop(0, pairs, two_groups, 0)
    arrange(half_b, kind_b, tile_b)
    deposit(2 * pairs - 2, tile_a)
    deposit(2 * pairs - 1, tile_b)
    deposit_rest(2 * pairs - 1, tile_b)

    def out_copy(k):
        return pltpu.make_async_copy(out_ref.at[k], out_any.at[k], out_sems.at[k])

    def two_planes(pair, carry):
        combine(2 * pair, grid_ref, plane_ref)
        for i in range(2):
            encode(plane_ref.at[i], out_ref.at[2 * pair + i])
            out_copy(2 * pair + i).start()
        return carry

    lax.fori_loop(0, KZ // 2, two_planes, 0)
    for k in range(KZ):
        out_copy(k).wait()


def combine(k, grid_ref, plane_ref):
    lane = lax.broadcasted_iota(jnp.int32, (8, 128), 1)
    z = ((lane >> 6) << 2) + ((lane >> 3) & 3)
    z_kept = z < 6
    z_past = z < 2
    y_kept = (lane & 7) < 6
    y_past = (lane & 7) < 2
    last_k = lax.rem(k + KZ - 1, KZ)
    third_k = lax.rem(k + 2, KZ)

    def slabs(odd, row):
        def at(copy, plane):
            return grid_ref[pl.ds(pl.multiple_of(FRONT + (copy * KZ + plane) * PLANE + row, 8), 8), :]

        even = [at(odd, p) for p in (k, k + 1, third_k)]
        odd = [at(2 + odd, p) for p in (last_k, k, k + 1)]
        return [jnp.where(z_kept, even[i], even[i + 1]) + jnp.where(z_past, odd[i], odd[i + 1]) for i in range(2)]

    def put_ends(i, below, above, value):
        plane_ref[i, pl.ds(TAIL + below, 1), :] = value[7:8]
        plane_ref[i, pl.ds(TAIL + 40 + above, 1), :] = value[0:1]

    def one_slab(v, carry):
        evens, odds = carry
        place = jnp.where(v == 0, 32, v - 1)
        above = jnp.where(v < 2, 33 - v, v - 2)
        new_evens, new_odds = [], []
        for part in range(3):
            row = v * UROWS + 8 * part
            even, odd = slabs(0, row), slabs(1, row - UROWS)
            for i in range(2):
                value = jnp.where(y_kept, evens[part][i], even[i]) + jnp.where(y_past, odds[part][i], odd[i])
                if part == 0:
                    put_ends(i, place, above, value)
                else:
                    plane_ref[i, pl.ds(pl.multiple_of(place * 16 + 8 * part - 8, 8), 8), :] = value
            new_evens.append(even)
            new_odds.append(odd)
        return new_evens, new_odds

    zero = jnp.zeros((8, 128), jnp.float32)
    start = [[zero] * 2] * 3
    evens, odds = lax.fori_loop(0, 33, one_slab, (start, start), unroll=UNROLL)
    odd = slabs(1, 32 * UROWS)
    for i in range(2):
        for part in (1, 2):
            begin = EDGE + 8 * part - 8
            plane_ref[i, begin : begin + 8, :] += jnp.where(y_past, odds[part][i], 0.0)
        value = jnp.where(y_kept, evens[0][i], 0.0) + jnp.where(y_past, odds[0][i], odd[i])
        plane_ref[i, TAIL + 32 : TAIL + 33, :] += value[7:8]
        plane_ref[i, TAIL + 71 : TAIL + 72, :] = value[0:1]
        plane_ref[i, TAIL + 72 : TAIL + 73, :] += jnp.where(y_past, odd[i], 0.0)[0:1]


def encode(plane_ref, out_ref):
    line = lax.broadcasted_iota(jnp.int32, (8, 128), 0)
    top = jnp.max(jnp.abs(plane_ref[: TAIL + 33, :]), axis=0, keepdims=True)
    top = jnp.maximum(top, jnp.max(jnp.abs(plane_ref[TAIL + 40 : TAIL + 73, :]), axis=0, keepdims=True))
    power = jnp.ceil(jnp.log2(jnp.maximum(top, 1e-37)) * 16.0 + 0.01)
    shrink = jnp.exp2(power * -0.0625)
    whole = jnp.round(plane_ref[...] * shrink * LEVELS)
    out_ref[...] = whole.astype(jnp.int32).astype(out_ref.dtype)
    begin = SCALE_ROW // 16 * 16
    marked = jnp.round(plane_ref[begin : begin + 8, :] * shrink * LEVELS)
    marked = jnp.where(line == SCALE_ROW - begin, power, marked)
    rest = jnp.round(plane_ref[begin + 8 : begin + 16, :] * shrink * LEVELS)
    out_ref[begin : begin + 16, :] = jnp.concatenate([marked, rest], axis=0).astype(jnp.int32).astype(out_ref.dtype)


def take_tails(tails, tail_ref, grow_ref):
    for src in range(16):
        tail = jnp.concatenate([t[src] for t in tails], axis=0).astype(jnp.float32)
        grow = jnp.exp2(tail[SCALE_ROW - TAIL : SCALE_ROW - TAIL + 1] * 0.0625) / LEVELS
        grow_ref[src * 8 : src * 8 + 8, :] = jnp.broadcast_to(grow, (8, 128))
        tail_ref[src * 80 : (src + 1) * 80, :] = tail * grow


def turn(rows_of, slabs, tail_ref, grow_ref, turn_ref):
    lane = lax.broadcasted_iota(jnp.int32, (8, 128), 1)
    line = lax.broadcasted_iota(jnp.int32, (8, 128), 0)
    for src in range(16):
        grow = grow_ref[src * 8 : src * 8 + 8, :]
        halves = []
        for which in range(len(slabs)):
            both = rows_of(src, which).astype(jnp.float32)
            above = tail_ref[pl.ds((src + 1) % 16 * 80 + slabs[which], 1), :]
            below = tail_ref[pl.ds((src + 15) % 16 * 80 + 40 + slabs[which], 1), :]
            upper = both[0:8] * grow + jnp.where(line == 0, below, 0.0)
            lower = both[8:16] * grow + jnp.where(line == 7, above, 0.0)
            halves.append((upper, lower))
        if len(slabs) == 1:
            halves.append((jnp.zeros((8, 128), jnp.float32),) * 2)
        for half in range(2):
            da, db = halves[0][half], halves[1][half]
            begin = src * 32 + half * 16
            turn_ref[pl.ds(begin, 8, stride=2), :] = jnp.where(lane & 32 == 0, da, pltpu.roll(db, 32, 1))
            turn_ref[pl.ds(begin + 1, 8, stride=2), :] = jnp.where(lane & 32 == 0, pltpu.roll(da, 96, 1), db)
    blocks = []
    for c in range(4):
        block = turn_ref[c * 128 : (c + 1) * 128, :].T.reshape(2, 2, 4, 8, 128)
        blocks.append([jnp.concatenate([block[0, which], block[1, which]], axis=0) for which in range(2)])
    return blocks


def edge_kernel(x_ref, *refs):
    tails, (down_ref, up_ref), scratch = refs[:5], refs[5:7], refs[7:]
    take_tails(tails, *scratch[:2])
    blocks = turn(lambda src, which: x_ref[src], (32,), *scratch[:2], scratch[2].at[0])
    for c, block in enumerate(blocks):
        down_ref[:, :, c * 128 : (c + 1) * 128] = block[0][:, 6:8]
        up_ref[:, :, c * 128 : (c + 1) * 128] = block[0][:, 0:2]


def assemble(x_ref, first, out_ref, scratch):
    tail_ref, grow_ref, turn_refs = scratch
    for pair in range(2):
        rows_of = lambda src, which: x_ref[src, (2 * pair + which) * 16 : (2 * pair + which + 1) * 16, :]
        slabs = (first + 2 * pair, first + 2 * pair + 1)
        blocks = turn(rows_of, slabs, tail_ref, grow_ref, turn_refs.at[pair])
        for c, block in enumerate(blocks):
            for which in range(2):
                begin = pair * 16 + which * 8
                out_ref[:, begin : begin + 8, c * 128 : (c + 1) * 128] = block[which]


def inner_kernel(x_ref, *refs):
    tails, out_ref, scratch = refs[:5], refs[5], refs[6:]
    step = pl.program_id(0)

    @pl.when(step == 0)
    def _():
        take_tails(tails, *scratch[:2])

    assemble(x_ref, 4 * step + 4, out_ref, scratch)


def outer_kernel(x_ref, *refs):
    tails, (below_ref, above_ref, _, out_ref), scratch = refs[:5], refs[5:9], refs[9:]
    step = pl.program_id(0)

    @pl.when(step == 0)
    def _():
        take_tails(tails, *scratch[:2])

    assemble(x_ref, 28 * step, out_ref, scratch)

    @pl.when(step == 0)
    def _():
        out_ref[:, 0:2, :] += below_ref[...]

    @pl.when(step == 1)
    def _():
        out_ref[:, 30:32, :] += above_ref[...]


def from_behind(block, axis, distance):
    devices = range(lax.axis_size(axis))
    route = [((i - distance) % len(devices), i) for i in devices]
    return lax.ppermute(block, axis, route)


def on_device(charges, weight_tiles, block_shape, block_box, live_blocks):
    nblk, atoms = charges.shape
    shapes_n, _, cells = weight_tiles.shape
    wflat = weight_tiles.reshape(shapes_n * atoms, cells)
    rows = (nblk // 128, 128)
    vmem = pl.BlockSpec(memory_space=pltpu.VMEM)
    smem = pl.BlockSpec(memory_space=pltpu.SMEM)
    hbm = pl.BlockSpec(memory_space=pl.ANY)
    sent = pl.pallas_call(
        spread_kernel,
        out_shape=jax.ShapeDtypeStruct((KZ, SENT, 128), WIRE),
        in_specs=[smem] + [vmem] * 3 + [hbm] * 2,
        out_specs=hbm,
        scratch_shapes=[
            pltpu.VMEM((GROWS + SPARE, 128), jnp.float32),
            pltpu.VMEM((shapes_n * atoms, cells), jnp.bfloat16),
            pltpu.VMEM((1024, 384), jnp.bfloat16),
            pltpu.VMEM((GROUP, shapes_n * atoms), jnp.bfloat16),
            pltpu.VMEM((GROUP, 1024), jnp.bfloat16),
            pltpu.VMEM((GROUP, 1024), jnp.bfloat16),
            pltpu.VMEM((GROUP, 128), jnp.float32),
            pltpu.VMEM((GROUP, 128), jnp.float32),
            pltpu.VMEM((GROUP * 4, 128), jnp.float32),
            pltpu.VMEM((GROUP * 4, 128), jnp.float32),
            pltpu.VMEM((2, SENT, 128), jnp.float32),
            pltpu.VMEM(rows, jnp.int32),
            pltpu.VMEM(rows, jnp.int32),
            pltpu.VMEM(rows, jnp.int32),
            pltpu.VMEM(rows, jnp.int32),
            pltpu.VMEM(rows, jnp.float32),
            pltpu.SMEM(rows, jnp.int32),
            pltpu.SMEM(rows, jnp.int32),
            pltpu.SMEM(rows, jnp.int32),
            pltpu.SMEM(rows, jnp.int32),
            pltpu.VMEM((KZ, SENT, 128), WIRE),
            pltpu.SemaphoreType.DMA((6,)),
            pltpu.SemaphoreType.DMA((KZ,)),
        ],
        compiler_params=pltpu.CompilerParams(vmem_limit_bytes=56 * 1024 * 1024),
        name="spread",
    )(
        live_blocks,
        charges,
        block_shape.reshape(rows),
        block_box.reshape(rows),
        wflat,
        jnp.asarray(restriction(), jnp.bfloat16),
    )
    got = lax.all_to_all(sent, "bx", split_axis=0, concat_axis=0, tiled=True)
    piece = lambda i: pl.BlockSpec((KZ, 16, 128), lambda p: (0, i, 0))
    tails = [piece(TAIL // 16 + i) for i in range(5)]
    small = pl.BlockSpec((8, 2, 512), lambda p: (0, 0, 0))
    full = jax.ShapeDtypeStruct((8, 256, 512), jnp.float32)
    scratch = [
        pltpu.VMEM((16 * 80, 128), jnp.float32),
        pltpu.VMEM((128, 128), jnp.float32),
        pltpu.VMEM((2, 512, 128), jnp.float32),
    ]
    params = pltpu.CompilerParams(vmem_limit_bytes=40 * 1024 * 1024)
    down, up = pl.pallas_call(
        edge_kernel,
        out_shape=(jax.ShapeDtypeStruct((8, 2, 512), jnp.float32),) * 2,
        grid=(1,),
        in_specs=[piece(EDGE // 16)] + tails,
        out_specs=(small, small),
        scratch_shapes=scratch,
        compiler_params=params,
        name="edge",
    )(*[got] * 6)
    below = from_behind(up, "by", 1)
    above = from_behind(down, "by", -1)
    inner = pl.pallas_call(
        inner_kernel,
        out_shape=full,
        grid=(6,),
        in_specs=[pl.BlockSpec((KZ, 64, 128), lambda p: (0, p + 1, 0))] + tails,
        out_specs=pl.BlockSpec((8, 32, 512), lambda p: (0, p + 1, 0)),
        scratch_shapes=scratch,
        compiler_params=params,
        name="inner",
    )(*[got] * 6)
    return pl.pallas_call(
        outer_kernel,
        out_shape=full,
        grid=(2,),
        in_specs=[pl.BlockSpec((KZ, 64, 128), lambda p: (0, 7 * p, 0))]
        + tails
        + [small, small, pl.BlockSpec(memory_space=pl.ANY)],
        out_specs=pl.BlockSpec((8, 32, 512), lambda p: (0, 7 * p, 0)),
        scratch_shapes=scratch,
        input_output_aliases={8: 0},
        compiler_params=params,
        name="outer",
    )(*[got] * 6, below, above, inner)


def solution(mesh):
    return jax.shard_map(
        on_device,
        mesh=mesh,
        in_specs=(P(("bx", "by"), None), P(), P(("bx", "by")), P(("bx", "by")), P(("bx", "by"))),
        out_specs=P("bx", "by", None),
        check_vma=False,
    )
```

```python
import functools

import jax
import jax.numpy as jnp
import numpy as np
from jax import lax
from jax.experimental import pallas as pl
from jax.experimental.pallas import tpu as pltpu
from jax.sharding import PartitionSpec as P

NZ = 128
GROUP = 256
BATCH = 8
KZ = 16
UROWS = 24
VSLOTS = 34
FRONT = VSLOTS * UROWS
PLANE = UROWS * VSLOTS
GROWS = FRONT + 4 * KZ * PLANE
SPARE = -GROWS % 256 + 256
DUMP = GROWS + SPARE - 8
EDGE = 512
TAIL = EDGE + 16
SENT = TAIL + 80
WIRE = jnp.int16
LEVELS = 32700.0
UNROLL = 11
SCALE_ROW = TAIL + 33


def restriction():
    coef = [1.0, 4.0, 6.0, 4.0, 1.0]
    table = np.zeros((2, 256, 256), np.float32)
    for p in range(8):
        for mm in range(6):
            tap = p + 4 - 2 * mm
            if not 0 <= tap < 5:
                continue
            side = p // 4
            near = mm - 2 * side
            for q in range(8):
                for r in range(8):
                    z, y = (r - 2) % 8, (q - 2) % 8
                    lane = z // 4 * 64 + near % 2 * 32 + z % 4 * 8 + y
                    table[side, (p % 4 * 8 + q) * 8 + r, near // 2 * 128 + lane] = coef[tap] / 8.0
    return np.concatenate([table, table], axis=1).reshape(1024, 256)


def place_blocks(shape_ref, box_ref, live, base_ref, fast_ref, first_ref, many_ref, code_ref):
    lane = lax.broadcasted_iota(jnp.int32, base_ref.shape, 1)
    slot = lax.broadcasted_iota(jnp.int32, base_ref.shape, 0) * 128 + lane
    box = box_ref[...]
    u = box >> 11
    v = (box >> 5) & 63
    w = box & 31
    kind = (w & 1) * 2 + (v & 1)
    base = FRONT + (kind * KZ + (w >> 1)) * PLANE + (v >> 1) * UROWS + 7 + u
    late = jnp.zeros(base.shape, jnp.int32)
    for d in range(1, BATCH):
        near = jnp.abs(base - pltpu.roll(base, d, 1)) < 3
        late = jnp.where(near & ((lane & (BATCH - 1)) >= d), 1, late)
    base_ref[...] = base
    fast_ref[...] = jnp.where(late == 1, DUMP, base)
    first = jnp.where(late == 1, lane & (BATCH - 1), BATCH)
    for d in (1, 2, 4):
        first = jnp.minimum(first, pltpu.roll(first, 128 - d, 1))
        late = late + pltpu.roll(late, 128 - d, 1)
    first_ref[...] = first
    many_ref[...] = jnp.where(late > 1, 1, 0)
    code = jnp.where(slot < live, shape_ref[...], 32) * 4 + kind
    code_ref[...] = code.astype(jnp.float32)


def spread_kernel(live_ref, q_ref, shape_ref, box_ref, w_any, r_any, out_any, *scratch):
    grid_ref, w_ref, r_ref, pick_ref, half_a, half_b, kind_a, kind_b, tile_a, tile_b, plane_ref = scratch[:11]
    base_v, fast_v, first_v, many_v, code_ref, base_ref, fast_ref, first_ref, many_ref = scratch[11:20]
    out_ref, sems, out_sems = scratch[20:]
    shapes_n = w_ref.shape[0] // 128
    copies = [pltpu.make_async_copy(w_any, w_ref, sems.at[0]), pltpu.make_async_copy(r_any, r_ref, sems.at[1])]
    for copy in copies:
        copy.start()
    place_blocks(shape_ref, box_ref, live_ref[0], base_v, fast_v, first_v, many_v, code_ref)
    places = ((base_v, base_ref), (fast_v, fast_ref), (first_v, first_ref), (many_v, many_ref))
    for i, (here, there) in enumerate(places):
        copies.append(pltpu.make_async_copy(here, there, sems.at[2 + i]))
        copies[-1].start()
    for ref in (half_b, kind_b):
        ref[...] = jnp.zeros(ref.shape, ref.dtype)

    def clear(step, carry):
        grid_ref[pl.ds(pl.multiple_of(step * 256, 256), 256), :] = jnp.zeros((256, 128), jnp.float32)
        return carry

    lax.fori_loop(0, (GROWS + SPARE) // 256, clear, 0)
    for copy in copies:
        copy.wait()

    def product(step, half_ref, kind_ref):
        begin = pl.multiple_of(step * GROUP, GROUP)
        qg = q_ref[pl.ds(begin, GROUP), :]
        codes = [code_ref[pl.ds(step * (GROUP // 128) + h, 1), :] for h in range(GROUP // 128)]
        code = jnp.concatenate([jnp.broadcast_to(c, (128, 128)).T for c in codes], axis=0)
        whole = jnp.floor(code * 0.25)
        sg = whole.astype(jnp.bfloat16)
        kind_ref[...] = code - 4.0 * whole
        part = jnp.zeros((GROUP, 512), jnp.float32)
        for s in range(0, shapes_n, 2):
            pick = jnp.concatenate([jnp.where(sg == s + i, qg, jnp.zeros_like(qg)) for i in range(2)], axis=1)
            part += jnp.dot(pick, w_ref[s * 128 : (s + 2) * 128, :], preferred_element_type=jnp.float32)
        high = part.astype(jnp.bfloat16)
        low = (part - high.astype(jnp.float32)).astype(jnp.bfloat16)
        for side in range(2):
            half_ref[:, side * 512 : side * 512 + 256] = high[:, side * 256 : side * 256 + 256]
            half_ref[:, side * 512 + 256 : side * 512 + 512] = low[:, side * 256 : side * 256 + 256]

    def arrange(half_ref, kind_ref, tile_ref):
        near, far = [
            jnp.dot(half_ref[:, c : c + 512], r_ref[c : c + 512, :], preferred_element_type=jnp.float32)
            for c in (0, 512)
        ]
        cells = [near[:, :128], near[:, 128:] + far[:, :128], far[:, 128:]]
        kind = kind_ref[...]
        z_odd = kind >= 2.0
        y_odd = (kind == 1.0) | (kind == 3.0)
        y_upper = (lax.broadcasted_iota(jnp.int32, kind.shape, 1) & 4) != 0
        for du in range(3):
            rows = cells[du]
            rows = jnp.where(z_odd, pltpu.roll(rows, 64, 1), rows)
            crossed = jnp.where(y_upper, pltpu.roll(rows, 4, 1), pltpu.roll(rows, 124, 1))
            tile_ref[pl.ds(du, GROUP, stride=4), :] = jnp.where(y_odd, crossed, rows)

    def at(ref, step, i):
        return ref[step * (GROUP // 128) + i // 128, i % 128]

    def deposit(step, tile_ref):
        for batch in range(GROUP // BATCH):
            slots = [batch * BATCH + j for j in range(BATCH)]
            rows = [at(fast_ref, step, i) for i in slots]
            sums = [grid_ref[pl.ds(r, 3), :] + tile_ref[4 * i : 4 * i + 3, :] for r, i in zip(rows, slots)]
            for r, value in zip(rows, sums):
                grid_ref[pl.ds(r, 3), :] = value

    def deposit_rest(step, tile_ref):
        heads = range(0, GROUP, BATCH)
        firsts = [at(first_ref, step, i) for i in heads]

        @pl.when(functools.reduce(jnp.minimum, firsts) < BATCH)
        def _():
            for i, first in zip(heads, firsts):
                held = jnp.minimum(first, BATCH - 1)
                spot = base_ref[step * (GROUP // 128) + i // 128, i % 128 + held]
                spot = jnp.where(first < BATCH, spot, DUMP)
                grid_ref[pl.ds(spot, 3), :] += tile_ref[pl.ds((i + held) * 4, 3), :]

        @pl.when(functools.reduce(jnp.maximum, [at(many_ref, step, i) for i in heads]) > 0)
        def _():
            def one_batch(batch, carry):
                row = step * (GROUP // 128) + batch // (128 // BATCH)
                head = batch % (128 // BATCH) * BATCH

                @pl.when(many_ref[row, head] != 0)
                def _():
                    def one_block(j, inner):
                        spot = base_ref[row, head + j]

                        @pl.when((fast_ref[row, head + j] != spot) & (first_ref[row, head] != j))
                        def _():
                            grid_ref[pl.ds(spot, 3), :] += tile_ref[pl.ds((batch * BATCH + j) * 4, 3), :]

                        return inner

                    lax.fori_loop(0, BATCH, one_block, 0)

                return carry

            lax.fori_loop(0, GROUP // BATCH, one_batch, 0)

    def two_groups(pair, carry):
        step = 2 * pair
        arrange(half_b, kind_b, tile_b)
        product(step, half_a, kind_a)
        deposit(jnp.maximum(step - 1, 0), tile_b)
        arrange(half_a, kind_a, tile_a)
        product(step + 1, half_b, kind_b)
        deposit(step, tile_a)

        @pl.when(pair > 0)
        def _():
            deposit_rest(step - 1, tile_b)

        deposit_rest(step, tile_a)
        return carry

    pairs = (live_ref[0] + 2 * GROUP - 1) // (2 * GROUP)
    lax.fori_loop(0, pairs, two_groups, 0)
    arrange(half_b, kind_b, tile_b)
    deposit(2 * pairs - 1, tile_b)
    deposit_rest(2 * pairs - 1, tile_b)

    def out_copy(k):
        return pltpu.make_async_copy(out_ref.at[k], out_any.at[k], out_sems.at[k])

    def two_planes(pair, carry):
        combine(2 * pair, grid_ref, plane_ref)
        for i in range(2):
            encode(plane_ref.at[i], out_ref.at[2 * pair + i])
            out_copy(2 * pair + i).start()
        return carry

    lax.fori_loop(0, KZ // 2, two_planes, 0)
    for k in range(KZ):
        out_copy(k).wait()


def combine(k, grid_ref, plane_ref):
    lane = lax.broadcasted_iota(jnp.int32, (8, 128), 1)
    z = ((lane >> 6) << 2) + ((lane >> 3) & 3)
    z_kept = z < 6
    z_past = z < 2
    y_kept = (lane & 7) < 6
    y_past = (lane & 7) < 2
    last_k = lax.rem(k + KZ - 1, KZ)
    third_k = lax.rem(k + 2, KZ)

    def slabs(odd, row):
        def at(copy, plane):
            return grid_ref[pl.ds(pl.multiple_of(FRONT + (copy * KZ + plane) * PLANE + row, 8), 8), :]

        even = [at(odd, p) for p in (k, k + 1, third_k)]
        odd = [at(2 + odd, p) for p in (last_k, k, k + 1)]
        return [jnp.where(z_kept, even[i], even[i + 1]) + jnp.where(z_past, odd[i], odd[i + 1]) for i in range(2)]

    def put_ends(i, below, above, value):
        plane_ref[i, pl.ds(TAIL + below, 1), :] = value[7:8]
        plane_ref[i, pl.ds(TAIL + 40 + above, 1), :] = value[0:1]

    def one_slab(v, carry):
        evens, odds = carry
        place = jnp.where(v == 0, 32, v - 1)
        above = jnp.where(v < 2, 33 - v, v - 2)
        new_evens, new_odds = [], []
        for part in range(3):
            row = v * UROWS + 8 * part
            even, odd = slabs(0, row), slabs(1, row - UROWS)
            for i in range(2):
                value = jnp.where(y_kept, evens[part][i], even[i]) + jnp.where(y_past, odds[part][i], odd[i])
                if part == 0:
                    put_ends(i, place, above, value)
                else:
                    plane_ref[i, pl.ds(pl.multiple_of(place * 16 + 8 * part - 8, 8), 8), :] = value
            new_evens.append(even)
            new_odds.append(odd)
        return new_evens, new_odds

    zero = jnp.zeros((8, 128), jnp.float32)
    start = [[zero] * 2] * 3
    evens, odds = lax.fori_loop(0, 33, one_slab, (start, start), unroll=UNROLL)
    odd = slabs(1, 32 * UROWS)
    for i in range(2):
        for part in (1, 2):
            begin = EDGE + 8 * part - 8
            plane_ref[i, begin : begin + 8, :] += jnp.where(y_past, odds[part][i], 0.0)
        value = jnp.where(y_kept, evens[0][i], 0.0) + jnp.where(y_past, odds[0][i], odd[i])
        plane_ref[i, TAIL + 32 : TAIL + 33, :] += value[7:8]
        plane_ref[i, TAIL + 71 : TAIL + 72, :] = value[0:1]
        plane_ref[i, TAIL + 72 : TAIL + 73, :] += jnp.where(y_past, odd[i], 0.0)[0:1]


def encode(plane_ref, out_ref):
    line = lax.broadcasted_iota(jnp.int32, (8, 128), 0)
    top = jnp.max(jnp.abs(plane_ref[: TAIL + 33, :]), axis=0, keepdims=True)
    top = jnp.maximum(top, jnp.max(jnp.abs(plane_ref[TAIL + 40 : TAIL + 73, :]), axis=0, keepdims=True))
    power = jnp.ceil(jnp.log2(jnp.maximum(top, 1e-37)) * 16.0 + 0.01)
    shrink = jnp.exp2(power * -0.0625)
    whole = jnp.round(plane_ref[...] * shrink * LEVELS)
    out_ref[...] = whole.astype(jnp.int32).astype(out_ref.dtype)
    begin = SCALE_ROW // 16 * 16
    marked = jnp.round(plane_ref[begin : begin + 8, :] * shrink * LEVELS)
    marked = jnp.where(line == SCALE_ROW - begin, power, marked)
    rest = jnp.round(plane_ref[begin + 8 : begin + 16, :] * shrink * LEVELS)
    out_ref[begin : begin + 16, :] = jnp.concatenate([marked, rest], axis=0).astype(jnp.int32).astype(out_ref.dtype)


def take_tails(tails, tail_ref, grow_ref):
    for src in range(16):
        tail = jnp.concatenate([t[src] for t in tails], axis=0).astype(jnp.float32)
        grow = jnp.exp2(tail[SCALE_ROW - TAIL : SCALE_ROW - TAIL + 1] * 0.0625) / LEVELS
        grow_ref[src * 8 : src * 8 + 8, :] = jnp.broadcast_to(grow, (8, 128))
        tail_ref[src * 80 : (src + 1) * 80, :] = tail * grow


def turn(rows_of, slabs, tail_ref, grow_ref, turn_ref):
    lane = lax.broadcasted_iota(jnp.int32, (8, 128), 1)
    line = lax.broadcasted_iota(jnp.int32, (8, 128), 0)
    for src in range(16):
        grow = grow_ref[src * 8 : src * 8 + 8, :]
        halves = []
        for which in range(len(slabs)):
            both = rows_of(src, which).astype(jnp.float32)
            above = tail_ref[pl.ds((src + 1) % 16 * 80 + slabs[which], 1), :]
            below = tail_ref[pl.ds((src + 15) % 16 * 80 + 40 + slabs[which], 1), :]
            upper = both[0:8] * grow + jnp.where(line == 0, below, 0.0)
            lower = both[8:16] * grow + jnp.where(line == 7, above, 0.0)
            halves.append((upper, lower))
        if len(slabs) == 1:
            halves.append((jnp.zeros((8, 128), jnp.float32),) * 2)
        for half in range(2):
            da, db = halves[0][half], halves[1][half]
            begin = src * 32 + half * 16
            turn_ref[pl.ds(begin, 8, stride=2), :] = jnp.where(lane & 32 == 0, da, pltpu.roll(db, 32, 1))
            turn_ref[pl.ds(begin + 1, 8, stride=2), :] = jnp.where(lane & 32 == 0, pltpu.roll(da, 96, 1), db)
    blocks = []
    for c in range(4):
        block = turn_ref[c * 128 : (c + 1) * 128, :].T.reshape(2, 2, 4, 8, 128)
        blocks.append([jnp.concatenate([block[0, which], block[1, which]], axis=0) for which in range(2)])
    return blocks


def edge_kernel(x_ref, *refs):
    tails, (down_ref, up_ref), scratch = refs[:5], refs[5:7], refs[7:]
    take_tails(tails, *scratch[:2])
    blocks = turn(lambda src, which: x_ref[src], (32,), *scratch[:2], scratch[2].at[0])
    for c, block in enumerate(blocks):
        down_ref[:, :, c * 128 : (c + 1) * 128] = block[0][:, 6:8]
        up_ref[:, :, c * 128 : (c + 1) * 128] = block[0][:, 0:2]


def assemble(x_ref, first, out_ref, scratch):
    tail_ref, grow_ref, turn_refs = scratch
    for pair in range(2):
        rows_of = lambda src, which: x_ref[src, (2 * pair + which) * 16 : (2 * pair + which + 1) * 16, :]
        slabs = (first + 2 * pair, first + 2 * pair + 1)
        blocks = turn(rows_of, slabs, tail_ref, grow_ref, turn_refs.at[pair])
        for c, block in enumerate(blocks):
            for which in range(2):
                begin = pair * 16 + which * 8
                out_ref[:, begin : begin + 8, c * 128 : (c + 1) * 128] = block[which]


def inner_kernel(x_ref, *refs):
    tails, out_ref, scratch = refs[:5], refs[5], refs[6:]
    step = pl.program_id(0)

    @pl.when(step == 0)
    def _():
        take_tails(tails, *scratch[:2])

    assemble(x_ref, 4 * step + 4, out_ref, scratch)


def outer_kernel(x_ref, *refs):
    tails, (below_ref, above_ref, _, out_ref), scratch = refs[:5], refs[5:9], refs[9:]
    step = pl.program_id(0)

    @pl.when(step == 0)
    def _():
        take_tails(tails, *scratch[:2])

    assemble(x_ref, 28 * step, out_ref, scratch)

    @pl.when(step == 0)
    def _():
        out_ref[:, 0:2, :] += below_ref[...]

    @pl.when(step == 1)
    def _():
        out_ref[:, 30:32, :] += above_ref[...]


def from_behind(block, axis, distance):
    devices = range(lax.axis_size(axis))
    route = [((i - distance) % len(devices), i) for i in devices]
    return lax.ppermute(block, axis, route)


def on_device(charges, weight_tiles, block_shape, block_box, live_blocks):
    nblk, atoms = charges.shape
    shapes_n, _, cells = weight_tiles.shape
    wflat = weight_tiles.reshape(shapes_n * atoms, cells)
    rows = (nblk // 128, 128)
    vmem = pl.BlockSpec(memory_space=pltpu.VMEM)
    smem = pl.BlockSpec(memory_space=pltpu.SMEM)
    hbm = pl.BlockSpec(memory_space=pl.ANY)
    sent = pl.pallas_call(
        spread_kernel,
        out_shape=jax.ShapeDtypeStruct((KZ, SENT, 128), WIRE),
        in_specs=[smem] + [vmem] * 3 + [hbm] * 2,
        out_specs=hbm,
        scratch_shapes=[
            pltpu.VMEM((GROWS + SPARE, 128), jnp.float32),
            pltpu.VMEM((shapes_n * atoms, cells), jnp.bfloat16),
            pltpu.VMEM((1024, 256), jnp.bfloat16),
            pltpu.VMEM((GROUP, shapes_n * atoms), jnp.bfloat16),
            pltpu.VMEM((GROUP, 1024), jnp.bfloat16),
            pltpu.VMEM((GROUP, 1024), jnp.bfloat16),
            pltpu.VMEM((GROUP, 128), jnp.float32),
            pltpu.VMEM((GROUP, 128), jnp.float32),
            pltpu.VMEM((GROUP * 4, 128), jnp.float32),
            pltpu.VMEM((GROUP * 4, 128), jnp.float32),
            pltpu.VMEM((2, SENT, 128), jnp.float32),
            pltpu.VMEM(rows, jnp.int32),
            pltpu.VMEM(rows, jnp.int32),
            pltpu.VMEM(rows, jnp.int32),
            pltpu.VMEM(rows, jnp.int32),
            pltpu.VMEM(rows, jnp.float32),
            pltpu.SMEM(rows, jnp.int32),
            pltpu.SMEM(rows, jnp.int32),
            pltpu.SMEM(rows, jnp.int32),
            pltpu.SMEM(rows, jnp.int32),
            pltpu.VMEM((KZ, SENT, 128), WIRE),
            pltpu.SemaphoreType.DMA((6,)),
            pltpu.SemaphoreType.DMA((KZ,)),
        ],
        compiler_params=pltpu.CompilerParams(vmem_limit_bytes=56 * 1024 * 1024),
        name="spread",
    )(
        live_blocks,
        charges,
        block_shape.reshape(rows),
        block_box.reshape(rows),
        wflat,
        jnp.asarray(restriction(), jnp.bfloat16),
    )
    got = lax.all_to_all(sent, "bx", split_axis=0, concat_axis=0, tiled=True)
    piece = lambda i: pl.BlockSpec((KZ, 16, 128), lambda p: (0, i, 0))
    tails = [piece(TAIL // 16 + i) for i in range(5)]
    small = pl.BlockSpec((8, 2, 512), lambda p: (0, 0, 0))
    full = jax.ShapeDtypeStruct((8, 256, 512), jnp.float32)
    scratch = [
        pltpu.VMEM((16 * 80, 128), jnp.float32),
        pltpu.VMEM((128, 128), jnp.float32),
        pltpu.VMEM((2, 512, 128), jnp.float32),
    ]
    params = pltpu.CompilerParams(vmem_limit_bytes=40 * 1024 * 1024)
    down, up = pl.pallas_call(
        edge_kernel,
        out_shape=(jax.ShapeDtypeStruct((8, 2, 512), jnp.float32),) * 2,
        grid=(1,),
        in_specs=[piece(EDGE // 16)] + tails,
        out_specs=(small, small),
        scratch_shapes=scratch,
        compiler_params=params,
        name="edge",
    )(*[got] * 6)
    below = from_behind(up, "by", 1)
    above = from_behind(down, "by", -1)
    inner = pl.pallas_call(
        inner_kernel,
        out_shape=full,
        grid=(6,),
        in_specs=[pl.BlockSpec((KZ, 64, 128), lambda p: (0, p + 1, 0))] + tails,
        out_specs=pl.BlockSpec((8, 32, 512), lambda p: (0, p + 1, 0)),
        scratch_shapes=scratch,
        compiler_params=params,
        name="inner",
    )(*[got] * 6)
    return pl.pallas_call(
        outer_kernel,
        out_shape=full,
        grid=(2,),
        in_specs=[pl.BlockSpec((KZ, 64, 128), lambda p: (0, 7 * p, 0))]
        + tails
        + [small, small, pl.BlockSpec(memory_space=pl.ANY)],
        out_specs=pl.BlockSpec((8, 32, 512), lambda p: (0, 7 * p, 0)),
        scratch_shapes=scratch,
        input_output_aliases={8: 0},
        compiler_params=params,
        name="outer",
    )(*[got] * 6, below, above, inner)


def solution(mesh):
    return jax.shard_map(
        on_device,
        mesh=mesh,
        in_specs=(P(("bx", "by"), None), P(), P(("bx", "by")), P(("bx", "by")), P(("bx", "by"))),
        out_specs=P("bx", "by", None),
        check_vma=False,
    )
```

```python
import functools

import jax
import jax.numpy as jnp
import numpy as np
from jax import lax
from jax.experimental import pallas as pl
from jax.experimental.pallas import tpu as pltpu
from jax.sharding import PartitionSpec as P

NZ = 128
GROUP = 256
BATCH = 8
KZ = 16
UROWS = 24
VSLOTS = 34
FRONT = VSLOTS * UROWS
PLANE = UROWS * VSLOTS
GROWS = FRONT + 4 * KZ * PLANE
SPARE = -GROWS % 256 + 256
DUMP = GROWS + SPARE - 8
EDGE = 512
TAIL = EDGE + 16
SENT = TAIL + 80
WIRE = jnp.int16
LEVELS = 32700.0
UNROLL = 11
SCALE_ROW = TAIL + 33


def restriction():
    coef = [1.0, 4.0, 6.0, 4.0, 1.0]
    table = np.zeros((2, 256, 256), np.float32)
    for p in range(8):
        for mm in range(6):
            tap = p + 4 - 2 * mm
            if not 0 <= tap < 5:
                continue
            side = p // 4
            near = mm - 2 * side
            for q in range(8):
                for r in range(8):
                    z, y = (r - 2) % 8, (q - 2) % 8
                    lane = z // 4 * 64 + near % 2 * 32 + z % 4 * 8 + y
                    table[side, (p % 4 * 8 + q) * 8 + r, near // 2 * 128 + lane] = coef[tap] / 8.0
    return np.concatenate([table, table], axis=1).reshape(1024, 256)


def place_blocks(shape_ref, box_ref, live, base_ref, fast_ref, first_ref, many_ref, code_ref):
    lane = lax.broadcasted_iota(jnp.int32, base_ref.shape, 1)
    slot = lax.broadcasted_iota(jnp.int32, base_ref.shape, 0) * 128 + lane
    box = box_ref[...]
    u = box >> 11
    v = (box >> 5) & 63
    w = box & 31
    kind = (w & 1) * 2 + (v & 1)
    base = FRONT + (kind * KZ + (w >> 1)) * PLANE + (v >> 1) * UROWS + 7 + u
    late = jnp.zeros(base.shape, jnp.int32)
    for d in range(1, BATCH):
        near = jnp.abs(base - pltpu.roll(base, d, 1)) < 3
        late = jnp.where(near & ((lane & (BATCH - 1)) >= d), 1, late)
    base_ref[...] = base
    fast_ref[...] = jnp.where(late == 1, DUMP, base)
    first = jnp.where(late == 1, lane & (BATCH - 1), BATCH)
    for d in (1, 2, 4):
        first = jnp.minimum(first, pltpu.roll(first, 128 - d, 1))
        late = late + pltpu.roll(late, 128 - d, 1)
    first_ref[...] = first
    many_ref[...] = jnp.where(late > 1, 1, 0)
    code = jnp.where(slot < live, shape_ref[...], 32) * 4 + kind
    code_ref[...] = code.astype(jnp.float32)


def spread_kernel(live_ref, q_ref, shape_ref, box_ref, w_any, r_any, out_any, *scratch):
    grid_ref, w_ref, r_ref, pick_ref, half_a, half_b, kind_a, kind_b, tile_a, tile_b, plane_ref = scratch[:11]
    base_v, fast_v, first_v, many_v, code_ref, base_ref, fast_ref, first_ref, many_ref = scratch[11:20]
    out_ref, sems, out_sems = scratch[20:]
    shapes_n = w_ref.shape[0] // 128
    copies = [pltpu.make_async_copy(w_any, w_ref, sems.at[0]), pltpu.make_async_copy(r_any, r_ref, sems.at[1])]
    for copy in copies:
        copy.start()
    place_blocks(shape_ref, box_ref, live_ref[0], base_v, fast_v, first_v, many_v, code_ref)
    places = ((base_v, base_ref), (fast_v, fast_ref), (first_v, first_ref), (many_v, many_ref))
    for i, (here, there) in enumerate(places):
        copies.append(pltpu.make_async_copy(here, there, sems.at[2 + i]))
        copies[-1].start()
    for ref in (half_b, kind_b):
        ref[...] = jnp.zeros(ref.shape, ref.dtype)

    def clear(step, carry):
        grid_ref[pl.ds(pl.multiple_of(step * 256, 256), 256), :] = jnp.zeros((256, 128), jnp.float32)
        return carry

    lax.fori_loop(0, (GROWS + SPARE) // 256, clear, 0)
    for copy in copies:
        copy.wait()

    def product(step, half_ref, kind_ref):
        begin = pl.multiple_of(step * GROUP, GROUP)
        qg = q_ref[pl.ds(begin, GROUP), :]
        codes = [code_ref[pl.ds(step * (GROUP // 128) + h, 1), :] for h in range(GROUP // 128)]
        code = jnp.concatenate([jnp.broadcast_to(c, (128, 128)).T for c in codes], axis=0)
        whole = jnp.floor(code * 0.25)
        sg = whole.astype(jnp.bfloat16)
        kind_ref[...] = code - 4.0 * whole
        part = jnp.zeros((GROUP, 512), jnp.float32)
        for s in range(0, shapes_n, 2):
            pick = jnp.concatenate([jnp.where(sg == s + i, qg, jnp.zeros_like(qg)) for i in range(2)], axis=1)
            part += jnp.dot(pick, w_ref[s * 128 : (s + 2) * 128, :], preferred_element_type=jnp.float32)
        high = part.astype(jnp.bfloat16)
        low = (part - high.astype(jnp.float32)).astype(jnp.bfloat16)
        for side in range(2):
            half_ref[:, side * 512 : side * 512 + 256] = high[:, side * 256 : side * 256 + 256]
            half_ref[:, side * 512 + 256 : side * 512 + 512] = low[:, side * 256 : side * 256 + 256]

    def arrange(half_ref, kind_ref, tile_ref):
        near, far = [
            jnp.dot(half_ref[:, c : c + 512], r_ref[c : c + 512, :], preferred_element_type=jnp.float32)
            for c in (0, 512)
        ]
        cells = [near[:, :128], near[:, 128:] + far[:, :128], far[:, 128:]]
        kind = kind_ref[...]
        z_odd = kind >= 2.0
        y_odd = (kind == 1.0) | (kind == 3.0)
        y_upper = (lax.broadcasted_iota(jnp.int32, kind.shape, 1) & 4) != 0
        for du in range(3):
            rows = cells[du]
            rows = jnp.where(z_odd, pltpu.roll(rows, 64, 1), rows)
            crossed = jnp.where(y_upper, pltpu.roll(rows, 4, 1), pltpu.roll(rows, 124, 1))
            tile_ref[pl.ds(du, GROUP, stride=4), :] = jnp.where(y_odd, crossed, rows)

    def at(ref, step, i):
        return ref[step * (GROUP // 128) + i // 128, i % 128]

    def deposit(step, tile_ref):
        for batch in range(GROUP // BATCH):
            slots = [batch * BATCH + j for j in range(BATCH)]
            rows = [at(fast_ref, step, i) for i in slots]
            sums = [grid_ref[pl.ds(r, 3), :] + tile_ref[4 * i : 4 * i + 3, :] for r, i in zip(rows, slots)]
            for r, value in zip(rows, sums):
                grid_ref[pl.ds(r, 3), :] = value

    def deposit_rest(step, tile_ref):
        heads = range(0, GROUP, BATCH)
        firsts = [at(first_ref, step, i) for i in heads]

        @pl.when(functools.reduce(jnp.minimum, firsts) < BATCH)
        def _():
            for i, first in zip(heads, firsts):
                held = jnp.minimum(first, BATCH - 1)
                spot = base_ref[step * (GROUP // 128) + i // 128, i % 128 + held]
                spot = jnp.where(first < BATCH, spot, DUMP)
                grid_ref[pl.ds(spot, 3), :] += tile_ref[pl.ds((i + held) * 4, 3), :]

        @pl.when(functools.reduce(jnp.maximum, [at(many_ref, step, i) for i in heads]) > 0)
        def _():
            def one_batch(batch, carry):
                row = step * (GROUP // 128) + batch // (128 // BATCH)
                head = batch % (128 // BATCH) * BATCH

                @pl.when(many_ref[row, head] != 0)
                def _():
                    def one_block(j, inner):
                        spot = base_ref[row, head + j]

                        @pl.when((fast_ref[row, head + j] != spot) & (first_ref[row, head] != j))
                        def _():
                            grid_ref[pl.ds(spot, 3), :] += tile_ref[pl.ds((batch * BATCH + j) * 4, 3), :]

                        return inner

                    lax.fori_loop(0, BATCH, one_block, 0)

                return carry

            lax.fori_loop(0, GROUP // BATCH, one_batch, 0)

    def two_groups(pair, carry):
        step = 2 * pair
        arrange(half_b, kind_b, tile_b)
        product(step, half_a, kind_a)
        deposit(jnp.maximum(step - 1, 0), tile_b)
        arrange(half_a, kind_a, tile_a)
        product(step + 1, half_b, kind_b)
        deposit(step, tile_a)

        @pl.when(pair > 0)
        def _():
            deposit_rest(step - 1, tile_b)

        deposit_rest(step, tile_a)
        return carry

    pairs = (live_ref[0] + 2 * GROUP - 1) // (2 * GROUP)
    lax.fori_loop(0, pairs, two_groups, 0)
    arrange(half_b, kind_b, tile_b)
    deposit(2 * pairs - 1, tile_b)
    deposit_rest(2 * pairs - 1, tile_b)

    def out_copy(k):
        return pltpu.make_async_copy(out_ref.at[k], out_any.at[k], out_sems.at[k])

    def two_planes(pair, carry):
        combine(2 * pair, grid_ref, plane_ref)
        for i in range(2):
            encode(plane_ref.at[i], out_ref.at[2 * pair + i])
            out_copy(2 * pair + i).start()
        return carry

    lax.fori_loop(0, KZ // 2, two_planes, 0)
    for k in range(KZ):
        out_copy(k).wait()


def combine(k, grid_ref, plane_ref):
    lane = lax.broadcasted_iota(jnp.int32, (8, 128), 1)
    z = ((lane >> 6) << 2) + ((lane >> 3) & 3)
    z_kept = z < 6
    z_past = z < 2
    y_kept = (lane & 7) < 6
    y_past = (lane & 7) < 2
    last_k = lax.rem(k + KZ - 1, KZ)
    third_k = lax.rem(k + 2, KZ)

    def slabs(odd, row):
        def at(copy, plane):
            return grid_ref[pl.ds(pl.multiple_of(FRONT + (copy * KZ + plane) * PLANE + row, 8), 8), :]

        even = [at(odd, p) for p in (k, k + 1, third_k)]
        odd = [at(2 + odd, p) for p in (last_k, k, k + 1)]
        return [jnp.where(z_kept, even[i], even[i + 1]) + jnp.where(z_past, odd[i], odd[i + 1]) for i in range(2)]

    def put_ends(i, below, above, value):
        plane_ref[i, pl.ds(TAIL + below, 1), :] = value[7:8]
        plane_ref[i, pl.ds(TAIL + 40 + above, 1), :] = value[0:1]

    def one_slab(v, carry):
        evens, odds = carry
        place = jnp.where(v == 0, 32, v - 1)
        above = jnp.where(v < 2, 33 - v, v - 2)
        new_evens, new_odds = [], []
        for part in range(3):
            row = v * UROWS + 8 * part
            even, odd = slabs(0, row), slabs(1, row - UROWS)
            for i in range(2):
                value = jnp.where(y_kept, evens[part][i], even[i]) + jnp.where(y_past, odds[part][i], odd[i])
                if part == 0:
                    put_ends(i, place, above, value)
                else:
                    plane_ref[i, pl.ds(pl.multiple_of(place * 16 + 8 * part - 8, 8), 8), :] = value
            new_evens.append(even)
            new_odds.append(odd)
        return new_evens, new_odds

    zero = jnp.zeros((8, 128), jnp.float32)
    start = [[zero] * 2] * 3
    evens, odds = lax.fori_loop(0, 33, one_slab, (start, start), unroll=UNROLL)
    odd = slabs(1, 32 * UROWS)
    for i in range(2):
        for part in (1, 2):
            begin = EDGE + 8 * part - 8
            plane_ref[i, begin : begin + 8, :] += jnp.where(y_past, odds[part][i], 0.0)
        value = jnp.where(y_kept, evens[0][i], 0.0) + jnp.where(y_past, odds[0][i], odd[i])
        plane_ref[i, TAIL + 32 : TAIL + 33, :] += value[7:8]
        plane_ref[i, TAIL + 71 : TAIL + 72, :] = value[0:1]
        plane_ref[i, TAIL + 72 : TAIL + 73, :] += jnp.where(y_past, odd[i], 0.0)[0:1]


def encode(plane_ref, out_ref):
    line = lax.broadcasted_iota(jnp.int32, (8, 128), 0)
    top = jnp.max(jnp.abs(plane_ref[: TAIL + 33, :]), axis=0, keepdims=True)
    top = jnp.maximum(top, jnp.max(jnp.abs(plane_ref[TAIL + 40 : TAIL + 73, :]), axis=0, keepdims=True))
    power = jnp.ceil(jnp.log2(jnp.maximum(top, 1e-37)) * 16.0 + 0.01)
    shrink = jnp.exp2(power * -0.0625)
    whole = jnp.round(plane_ref[...] * shrink * LEVELS)
    out_ref[...] = whole.astype(jnp.int32).astype(out_ref.dtype)
    begin = SCALE_ROW // 16 * 16
    marked = jnp.round(plane_ref[begin : begin + 8, :] * shrink * LEVELS)
    marked = jnp.where(line == SCALE_ROW - begin, power, marked)
    rest = jnp.round(plane_ref[begin + 8 : begin + 16, :] * shrink * LEVELS)
    out_ref[begin : begin + 16, :] = jnp.concatenate([marked, rest], axis=0).astype(jnp.int32).astype(out_ref.dtype)


def take_tails(x_ref, tail_ref, grow_ref):
    for src in range(16):
        tail = x_ref[src, TAIL:SENT, :].astype(jnp.float32)
        grow = jnp.exp2(tail[SCALE_ROW - TAIL : SCALE_ROW - TAIL + 1] * 0.0625) / LEVELS
        grow_ref[src * 8 : src * 8 + 8, :] = jnp.broadcast_to(grow, (8, 128))
        tail_ref[src * 80 : (src + 1) * 80, :] = tail * grow


def turn(rows_of, slabs, tail_ref, grow_ref, turn_ref):
    lane = lax.broadcasted_iota(jnp.int32, (8, 128), 1)
    line = lax.broadcasted_iota(jnp.int32, (8, 128), 0)
    for src in range(16):
        grow = grow_ref[src * 8 : src * 8 + 8, :]
        halves = []
        for which in range(len(slabs)):
            both = rows_of(src, which).astype(jnp.float32)
            above = tail_ref[pl.ds((src + 1) % 16 * 80 + slabs[which], 1), :]
            below = tail_ref[pl.ds((src + 15) % 16 * 80 + 40 + slabs[which], 1), :]
            upper = both[0:8] * grow + jnp.where(line == 0, below, 0.0)
            lower = both[8:16] * grow + jnp.where(line == 7, above, 0.0)
            halves.append((upper, lower))
        if len(slabs) == 1:
            halves.append((jnp.zeros((8, 128), jnp.float32),) * 2)
        for half in range(2):
            da, db = halves[0][half], halves[1][half]
            begin = src * 32 + half * 16
            turn_ref[pl.ds(begin, 8, stride=2), :] = jnp.where(lane & 32 == 0, da, pltpu.roll(db, 32, 1))
            turn_ref[pl.ds(begin + 1, 8, stride=2), :] = jnp.where(lane & 32 == 0, pltpu.roll(da, 96, 1), db)
    blocks = []
    for c in range(4):
        block = turn_ref[c * 128 : (c + 1) * 128, :].T.reshape(2, 2, 4, 8, 128)
        blocks.append([jnp.concatenate([block[0, which], block[1, which]], axis=0) for which in range(2)])
    return blocks


def edge_kernel(x_ref, *refs):
    (down_ref, up_ref), scratch = refs[:2], refs[2:]
    take_tails(x_ref, *scratch[:2])
    blocks = turn(lambda src, which: x_ref[src, EDGE:TAIL, :], (32,), *scratch[:2], scratch[2].at[0])
    for c, block in enumerate(blocks):
        down_ref[:, :, c * 128 : (c + 1) * 128] = block[0][:, 6:8]
        up_ref[:, :, c * 128 : (c + 1) * 128] = block[0][:, 0:2]


def assemble(x_ref, first, out_ref, scratch):
    tail_ref, grow_ref, turn_refs = scratch
    for pair in range(2):
        rows_of = lambda src, which: x_ref[src, pl.ds(pl.multiple_of((first + 2 * pair + which) * 16, 16), 16), :]
        slabs = (first + 2 * pair, first + 2 * pair + 1)
        blocks = turn(rows_of, slabs, tail_ref, grow_ref, turn_refs.at[pair])
        for c, block in enumerate(blocks):
            for which in range(2):
                begin = pair * 16 + which * 8
                out_ref[:, begin : begin + 8, c * 128 : (c + 1) * 128] = block[which]


def inner_kernel(x_ref, *refs):
    out_ref, scratch = refs[0], refs[1:]
    step = pl.program_id(0)

    @pl.when(step == 0)
    def _():
        take_tails(x_ref, *scratch[:2])

    assemble(x_ref, 4 * step + 4, out_ref, scratch)


def outer_kernel(x_ref, *refs):
    (below_ref, above_ref, _, out_ref), scratch = refs[:4], refs[4:]
    step = pl.program_id(0)

    @pl.when(step == 0)
    def _():
        take_tails(x_ref, *scratch[:2])

    assemble(x_ref, 28 * step, out_ref, scratch)

    @pl.when(step == 0)
    def _():
        out_ref[:, 0:2, :] += below_ref[...]

    @pl.when(step == 1)
    def _():
        out_ref[:, 30:32, :] += above_ref[...]


def from_behind(block, axis, distance):
    devices = range(lax.axis_size(axis))
    route = [((i - distance) % len(devices), i) for i in devices]
    return lax.ppermute(block, axis, route)


def on_device(charges, weight_tiles, block_shape, block_box, live_blocks):
    nblk, atoms = charges.shape
    shapes_n, _, cells = weight_tiles.shape
    wflat = weight_tiles.reshape(shapes_n * atoms, cells)
    rows = (nblk // 128, 128)
    vmem = pl.BlockSpec(memory_space=pltpu.VMEM)
    smem = pl.BlockSpec(memory_space=pltpu.SMEM)
    hbm = pl.BlockSpec(memory_space=pl.ANY)
    sent = pl.pallas_call(
        spread_kernel,
        out_shape=jax.ShapeDtypeStruct((KZ, SENT, 128), WIRE),
        in_specs=[smem] + [vmem] * 3 + [hbm] * 2,
        out_specs=hbm,
        scratch_shapes=[
            pltpu.VMEM((GROWS + SPARE, 128), jnp.float32),
            pltpu.VMEM((shapes_n * atoms, cells), jnp.bfloat16),
            pltpu.VMEM((1024, 256), jnp.bfloat16),
            pltpu.VMEM((GROUP, shapes_n * atoms), jnp.bfloat16),
            pltpu.VMEM((GROUP, 1024), jnp.bfloat16),
            pltpu.VMEM((GROUP, 1024), jnp.bfloat16),
            pltpu.VMEM((GROUP, 128), jnp.float32),
            pltpu.VMEM((GROUP, 128), jnp.float32),
            pltpu.VMEM((GROUP * 4, 128), jnp.float32),
            pltpu.VMEM((GROUP * 4, 128), jnp.float32),
            pltpu.VMEM((2, SENT, 128), jnp.float32),
            pltpu.VMEM(rows, jnp.int32),
            pltpu.VMEM(rows, jnp.int32),
            pltpu.VMEM(rows, jnp.int32),
            pltpu.VMEM(rows, jnp.int32),
            pltpu.VMEM(rows, jnp.float32),
            pltpu.SMEM(rows, jnp.int32),
            pltpu.SMEM(rows, jnp.int32),
            pltpu.SMEM(rows, jnp.int32),
            pltpu.SMEM(rows, jnp.int32),
            pltpu.VMEM((KZ, SENT, 128), WIRE),
            pltpu.SemaphoreType.DMA((6,)),
            pltpu.SemaphoreType.DMA((KZ,)),
        ],
        compiler_params=pltpu.CompilerParams(vmem_limit_bytes=56 * 1024 * 1024),
        name="spread",
    )(
        live_blocks,
        charges,
        block_shape.reshape(rows),
        block_box.reshape(rows),
        wflat,
        jnp.asarray(restriction(), jnp.bfloat16),
    )
    got = lax.all_to_all(sent, "bx", split_axis=0, concat_axis=0, tiled=True)
    small = pl.BlockSpec((8, 2, 512), lambda p: (0, 0, 0))
    full = jax.ShapeDtypeStruct((8, 256, 512), jnp.float32)
    scratch = [
        pltpu.VMEM((16 * 80, 128), jnp.float32),
        pltpu.VMEM((128, 128), jnp.float32),
        pltpu.VMEM((2, 512, 128), jnp.float32),
    ]
    params = pltpu.CompilerParams(vmem_limit_bytes=40 * 1024 * 1024)
    down, up = pl.pallas_call(
        edge_kernel,
        out_shape=(jax.ShapeDtypeStruct((8, 2, 512), jnp.float32),) * 2,
        grid=(1,),
        in_specs=[vmem],
        out_specs=(small, small),
        scratch_shapes=scratch,
        compiler_params=params,
        name="edge",
    )(got)
    below = from_behind(up, "by", 1)
    above = from_behind(down, "by", -1)
    inner = pl.pallas_call(
        inner_kernel,
        out_shape=full,
        grid=(6,),
        in_specs=[vmem],
        out_specs=pl.BlockSpec((8, 32, 512), lambda p: (0, p + 1, 0)),
        scratch_shapes=scratch,
        compiler_params=params,
        name="inner",
    )(got)
    return pl.pallas_call(
        outer_kernel,
        out_shape=full,
        grid=(2,),
        in_specs=[vmem, small, small, hbm],
        out_specs=pl.BlockSpec((8, 32, 512), lambda p: (0, 7 * p, 0)),
        scratch_shapes=scratch,
        input_output_aliases={3: 0},
        compiler_params=params,
        name="outer",
    )(got, below, above, inner)


def solution(mesh):
    return jax.shard_map(
        on_device,
        mesh=mesh,
        in_specs=(P(("bx", "by"), None), P(), P(("bx", "by")), P(("bx", "by")), P(("bx", "by"))),
        out_specs=P("bx", "by", None),
        check_vma=False,
    )
```

```python
import functools

import jax
import jax.numpy as jnp
import numpy as np
from jax import lax
from jax.experimental import pallas as pl
from jax.experimental.pallas import tpu as pltpu
from jax.sharding import PartitionSpec as P

NZ = 128
GROUP = 256
BATCH = 8
KZ = 16
UROWS = 24
VSLOTS = 34
FRONT = VSLOTS * UROWS
PLANE = UROWS * VSLOTS
GROWS = FRONT + 4 * KZ * PLANE
SPARE = -GROWS % 256 + 256
DUMP = GROWS + SPARE - 8
EDGE = 512
TAIL = EDGE + 16
SENT = TAIL + 80
WIRE = jnp.int16
LEVELS = 32700.0
UNROLL = 11
SCALE_ROW = TAIL + 33


def restriction():
    coef = [1.0, 4.0, 6.0, 4.0, 1.0]
    table = np.zeros((2, 256, 256), np.float32)
    for p in range(8):
        for mm in range(6):
            tap = p + 4 - 2 * mm
            if not 0 <= tap < 5:
                continue
            side = p // 4
            near = mm - 2 * side
            for q in range(8):
                for r in range(8):
                    z, y = (r - 2) % 8, (q - 2) % 8
                    lane = z // 4 * 64 + near % 2 * 32 + z % 4 * 8 + y
                    table[side, (p % 4 * 8 + q) * 8 + r, near // 2 * 128 + lane] = coef[tap] / 8.0
    return np.concatenate([table, table], axis=1).reshape(1024, 256)


def place_blocks(shape_ref, box_ref, live, base_ref, fast_ref, first_ref, many_ref, code_ref):
    lane = lax.broadcasted_iota(jnp.int32, base_ref.shape, 1)
    slot = lax.broadcasted_iota(jnp.int32, base_ref.shape, 0) * 128 + lane
    box = box_ref[...]
    u = box >> 11
    v = (box >> 5) & 63
    w = box & 31
    kind = (w & 1) * 2 + (v & 1)
    base = FRONT + (kind * KZ + (w >> 1)) * PLANE + (v >> 1) * UROWS + 7 + u
    late = jnp.zeros(base.shape, jnp.int32)
    for d in range(1, BATCH):
        near = jnp.abs(base - pltpu.roll(base, d, 1)) < 3
        late = jnp.where(near & ((lane & (BATCH - 1)) >= d), 1, late)
    base_ref[...] = base
    fast_ref[...] = jnp.where(late == 1, DUMP, base)
    first = jnp.where(late == 1, lane & (BATCH - 1), BATCH)
    for d in (1, 2, 4):
        first = jnp.minimum(first, pltpu.roll(first, 128 - d, 1))
        late = late + pltpu.roll(late, 128 - d, 1)
    first_ref[...] = first
    many_ref[...] = jnp.where(late > 1, 1, 0)
    code = jnp.where(slot < live, shape_ref[...], 32) * 4 + kind
    code_ref[...] = code.astype(jnp.float32)


def spread_kernel(live_ref, q_ref, shape_ref, box_ref, w_any, r_any, out_any, *scratch):
    grid_ref, w_ref, r_ref, pick_ref, half_a, half_b, kind_a, kind_b, tile_a, tile_b, plane_ref = scratch[:11]
    base_v, fast_v, first_v, many_v, code_ref, base_ref, fast_ref, first_ref, many_ref = scratch[11:20]
    out_ref, sems, out_sems = scratch[20:]
    shapes_n = w_ref.shape[0] // 128
    copies = [pltpu.make_async_copy(w_any, w_ref, sems.at[0]), pltpu.make_async_copy(r_any, r_ref, sems.at[1])]
    for copy in copies:
        copy.start()
    place_blocks(shape_ref, box_ref, live_ref[0], base_v, fast_v, first_v, many_v, code_ref)
    places = ((base_v, base_ref), (fast_v, fast_ref), (first_v, first_ref), (many_v, many_ref))
    for i, (here, there) in enumerate(places):
        copies.append(pltpu.make_async_copy(here, there, sems.at[2 + i]))
        copies[-1].start()
    for ref in (half_b, kind_b):
        ref[...] = jnp.zeros(ref.shape, ref.dtype)

    def clear(step, carry):
        grid_ref[pl.ds(pl.multiple_of(step * 256, 256), 256), :] = jnp.zeros((256, 128), jnp.float32)
        return carry

    lax.fori_loop(0, (GROWS + SPARE) // 256, clear, 0)
    for copy in copies:
        copy.wait()

    def product(step, half_ref, kind_ref):
        begin = pl.multiple_of(step * GROUP, GROUP)
        qg = q_ref[pl.ds(begin, GROUP), :]
        codes = [code_ref[pl.ds(step * (GROUP // 128) + h, 1), :] for h in range(GROUP // 128)]
        code = jnp.concatenate([jnp.broadcast_to(c, (128, 128)).T for c in codes], axis=0)
        whole = jnp.floor(code * 0.25)
        sg = whole.astype(jnp.bfloat16)
        kind_ref[...] = code - 4.0 * whole
        part = jnp.zeros((GROUP, 512), jnp.float32)
        for s in range(0, shapes_n, 2):
            pick = jnp.concatenate([jnp.where(sg == s + i, qg, jnp.zeros_like(qg)) for i in range(2)], axis=1)
            part += jnp.dot(pick, w_ref[s * 128 : (s + 2) * 128, :], preferred_element_type=jnp.float32)
        high = part.astype(jnp.bfloat16)
        low = (part - high.astype(jnp.float32)).astype(jnp.bfloat16)
        for side in range(2):
            half_ref[:, side * 512 : side * 512 + 256] = high[:, side * 256 : side * 256 + 256]
            half_ref[:, side * 512 + 256 : side * 512 + 512] = low[:, side * 256 : side * 256 + 256]

    def arrange(half_ref, kind_ref, tile_ref):
        near, far = [
            jnp.dot(half_ref[:, c : c + 512], r_ref[c : c + 512, :], preferred_element_type=jnp.float32)
            for c in (0, 512)
        ]
        cells = [near[:, :128], near[:, 128:] + far[:, :128], far[:, 128:]]
        kind = kind_ref[...]
        z_odd = kind >= 2.0
        y_odd = (kind == 1.0) | (kind == 3.0)
        y_upper = (lax.broadcasted_iota(jnp.int32, kind.shape, 1) & 4) != 0
        for du in range(3):
            rows = cells[du]
            rows = jnp.where(z_odd, pltpu.roll(rows, 64, 1), rows)
            crossed = jnp.where(y_upper, pltpu.roll(rows, 4, 1), pltpu.roll(rows, 124, 1))
            tile_ref[pl.ds(du, GROUP, stride=4), :] = jnp.where(y_odd, crossed, rows)

    def at(ref, step, i):
        return ref[step * (GROUP // 128) + i // 128, i % 128]

    def deposit(step, tile_ref):
        for batch in range(GROUP // BATCH):
            slots = [batch * BATCH + j for j in range(BATCH)]
            rows = [at(fast_ref, step, i) for i in slots]
            sums = [grid_ref[pl.ds(r, 3), :] + tile_ref[4 * i : 4 * i + 3, :] for r, i in zip(rows, slots)]
            for r, value in zip(rows, sums):
                grid_ref[pl.ds(r, 3), :] = value

    def deposit_rest(step, tile_ref):
        heads = range(0, GROUP, BATCH)
        firsts = [at(first_ref, step, i) for i in heads]

        @pl.when(functools.reduce(jnp.minimum, firsts) < BATCH)
        def _():
            for i, first in zip(heads, firsts):
                held = jnp.minimum(first, BATCH - 1)
                spot = base_ref[step * (GROUP // 128) + i // 128, i % 128 + held]
                spot = jnp.where(first < BATCH, spot, DUMP)
                grid_ref[pl.ds(spot, 3), :] += tile_ref[pl.ds((i + held) * 4, 3), :]

        @pl.when(functools.reduce(jnp.maximum, [at(many_ref, step, i) for i in heads]) > 0)
        def _():
            def one_batch(batch, carry):
                row = step * (GROUP // 128) + batch // (128 // BATCH)
                head = batch % (128 // BATCH) * BATCH

                @pl.when(many_ref[row, head] != 0)
                def _():
                    def one_block(j, inner):
                        spot = base_ref[row, head + j]

                        @pl.when((fast_ref[row, head + j] != spot) & (first_ref[row, head] != j))
                        def _():
                            grid_ref[pl.ds(spot, 3), :] += tile_ref[pl.ds((batch * BATCH + j) * 4, 3), :]

                        return inner

                    lax.fori_loop(0, BATCH, one_block, 0)

                return carry

            lax.fori_loop(0, GROUP // BATCH, one_batch, 0)

    def two_groups(pair, carry):
        step = 2 * pair
        arrange(half_b, kind_b, tile_b)
        product(step, half_a, kind_a)
        deposit(jnp.maximum(step - 1, 0), tile_b)
        arrange(half_a, kind_a, tile_a)
        product(step + 1, half_b, kind_b)
        deposit(step, tile_a)

        @pl.when(pair > 0)
        def _():
            deposit_rest(step - 1, tile_b)

        deposit_rest(step, tile_a)
        return carry

    pairs = (live_ref[0] + 2 * GROUP - 1) // (2 * GROUP)
    lax.fori_loop(0, pairs, two_groups, 0)
    arrange(half_b, kind_b, tile_b)
    deposit(2 * pairs - 1, tile_b)
    deposit_rest(2 * pairs - 1, tile_b)

    def out_copy(k):
        return pltpu.make_async_copy(out_ref.at[k], out_any.at[k], out_sems.at[k])

    def two_planes(pair, carry):
        combine(2 * pair, grid_ref, plane_ref)
        for i in range(2):
            encode(plane_ref.at[i], out_ref.at[2 * pair + i])
            out_copy(2 * pair + i).start()
        return carry

    lax.fori_loop(0, KZ // 2, two_planes, 0)
    for k in range(KZ):
        out_copy(k).wait()


def combine(k, grid_ref, plane_ref):
    lane = lax.broadcasted_iota(jnp.int32, (8, 128), 1)
    z = ((lane >> 6) << 2) + ((lane >> 3) & 3)
    z_kept = z < 6
    z_past = z < 2
    y_kept = (lane & 7) < 6
    y_past = (lane & 7) < 2
    last_k = lax.rem(k + KZ - 1, KZ)
    third_k = lax.rem(k + 2, KZ)

    def slabs(odd, row):
        def at(copy, plane):
            return grid_ref[pl.ds(pl.multiple_of(FRONT + (copy * KZ + plane) * PLANE + row, 8), 8), :]

        even = [at(odd, p) for p in (k, k + 1, third_k)]
        odd = [at(2 + odd, p) for p in (last_k, k, k + 1)]
        return [jnp.where(z_kept, even[i], even[i + 1]) + jnp.where(z_past, odd[i], odd[i + 1]) for i in range(2)]

    def put_ends(i, below, above, value):
        plane_ref[i, pl.ds(TAIL + below, 1), :] = value[7:8]
        plane_ref[i, pl.ds(TAIL + 40 + above, 1), :] = value[0:1]

    def one_slab(v, carry):
        evens, odds = carry
        place = jnp.where(v == 0, 32, v - 1)
        above = jnp.where(v < 2, 33 - v, v - 2)
        new_evens, new_odds = [], []
        for part in range(3):
            row = v * UROWS + 8 * part
            even, odd = slabs(0, row), slabs(1, row - UROWS)
            for i in range(2):
                value = jnp.where(y_kept, evens[part][i], even[i]) + jnp.where(y_past, odds[part][i], odd[i])
                if part == 0:
                    put_ends(i, place, above, value)
                else:
                    plane_ref[i, pl.ds(pl.multiple_of(place * 16 + 8 * part - 8, 8), 8), :] = value
            new_evens.append(even)
            new_odds.append(odd)
        return new_evens, new_odds

    zero = jnp.zeros((8, 128), jnp.float32)
    start = [[zero] * 2] * 3
    evens, odds = lax.fori_loop(0, 33, one_slab, (start, start), unroll=UNROLL)
    odd = slabs(1, 32 * UROWS)
    for i in range(2):
        for part in (1, 2):
            begin = EDGE + 8 * part - 8
            plane_ref[i, begin : begin + 8, :] += jnp.where(y_past, odds[part][i], 0.0)
        value = jnp.where(y_kept, evens[0][i], 0.0) + jnp.where(y_past, odds[0][i], odd[i])
        plane_ref[i, TAIL + 32 : TAIL + 33, :] += value[7:8]
        plane_ref[i, TAIL + 71 : TAIL + 72, :] = value[0:1]
        plane_ref[i, TAIL + 72 : TAIL + 73, :] += jnp.where(y_past, odd[i], 0.0)[0:1]


def encode(plane_ref, out_ref):
    line = lax.broadcasted_iota(jnp.int32, (8, 128), 0)
    top = jnp.max(jnp.abs(plane_ref[: TAIL + 33, :]), axis=0, keepdims=True)
    top = jnp.maximum(top, jnp.max(jnp.abs(plane_ref[TAIL + 40 : TAIL + 73, :]), axis=0, keepdims=True))
    power = jnp.ceil(jnp.log2(jnp.maximum(top, 1e-37)) * 16.0 + 0.01)
    shrink = jnp.exp2(power * -0.0625)
    whole = jnp.round(plane_ref[...] * shrink * LEVELS)
    out_ref[...] = whole.astype(jnp.int32).astype(out_ref.dtype)
    begin = SCALE_ROW // 16 * 16
    marked = jnp.round(plane_ref[begin : begin + 8, :] * shrink * LEVELS)
    marked = jnp.where(line == SCALE_ROW - begin, power, marked)
    rest = jnp.round(plane_ref[begin + 8 : begin + 16, :] * shrink * LEVELS)
    out_ref[begin : begin + 16, :] = jnp.concatenate([marked, rest], axis=0).astype(jnp.int32).astype(out_ref.dtype)


def take_tails(x_ref, tail_ref, grow_ref):
    for src in range(16):
        tail = x_ref[src, TAIL:SENT, :].astype(jnp.float32)
        grow = jnp.exp2(tail[SCALE_ROW - TAIL : SCALE_ROW - TAIL + 1] * 0.0625) / LEVELS
        grow_ref[src * 8 : src * 8 + 8, :] = jnp.broadcast_to(grow, (8, 128))
        tail_ref[src * 80 : (src + 1) * 80, :] = tail * grow


def turn(rows_of, slabs, tail_ref, grow_ref, turn_ref):
    lane = lax.broadcasted_iota(jnp.int32, (8, 128), 1)
    line = lax.broadcasted_iota(jnp.int32, (8, 128), 0)
    for src in range(16):
        grow = grow_ref[src * 8 : src * 8 + 8, :]
        halves = []
        for which in range(len(slabs)):
            both = rows_of(src, which).astype(jnp.float32)
            above = tail_ref[pl.ds((src + 1) % 16 * 80 + slabs[which], 1), :]
            below = tail_ref[pl.ds((src + 15) % 16 * 80 + 40 + slabs[which], 1), :]
            upper = both[0:8] * grow + jnp.where(line == 0, below, 0.0)
            lower = both[8:16] * grow + jnp.where(line == 7, above, 0.0)
            halves.append((upper, lower))
        if len(slabs) == 1:
            halves.append((jnp.zeros((8, 128), jnp.float32),) * 2)
        for half in range(2):
            da, db = halves[0][half], halves[1][half]
            begin = src * 32 + half * 16
            turn_ref[pl.ds(begin, 8, stride=2), :] = jnp.where(lane & 32 == 0, da, pltpu.roll(db, 32, 1))
            turn_ref[pl.ds(begin + 1, 8, stride=2), :] = jnp.where(lane & 32 == 0, pltpu.roll(da, 96, 1), db)
    blocks = []
    for c in range(4):
        block = turn_ref[c * 128 : (c + 1) * 128, :].T.reshape(2, 2, 4, 8, 128)
        blocks.append([jnp.concatenate([block[0, which], block[1, which]], axis=0) for which in range(2)])
    return blocks


def edge_kernel(x_ref, *refs):
    (down_ref, up_ref), scratch = refs[:2], refs[2:]
    take_tails(x_ref, *scratch[:2])
    blocks = turn(lambda src, which: x_ref[src, EDGE:TAIL, :], (32,), *scratch[:2], scratch[2].at[0])
    for c, block in enumerate(blocks):
        down_ref[:, :, c * 128 : (c + 1) * 128] = block[0][:, 6:8]
        up_ref[:, :, c * 128 : (c + 1) * 128] = block[0][:, 0:2]


def assemble(x_ref, first, out_ref, scratch):
    tail_ref, grow_ref, turn_refs = scratch
    for pair in range(4):
        rows_of = lambda src, which: x_ref[src, pl.ds(pl.multiple_of((first + 2 * pair + which) * 16, 16), 16), :]
        slabs = (first + 2 * pair, first + 2 * pair + 1)
        blocks = turn(rows_of, slabs, tail_ref, grow_ref, turn_refs.at[pair])
        for c, block in enumerate(blocks):
            for which in range(2):
                begin = pair * 16 + which * 8
                out_ref[:, begin : begin + 8, c * 128 : (c + 1) * 128] = block[which]


def inner_kernel(x_ref, *refs):
    out_ref, scratch = refs[0], refs[1:]
    step = pl.program_id(0)

    @pl.when(step == 0)
    def _():
        take_tails(x_ref, *scratch[:2])

    assemble(x_ref, 8 * step + 8, out_ref, scratch)


def outer_kernel(x_ref, *refs):
    (below_ref, above_ref, _, out_ref), scratch = refs[:4], refs[4:]
    step = pl.program_id(0)

    @pl.when(step == 0)
    def _():
        take_tails(x_ref, *scratch[:2])

    assemble(x_ref, 24 * step, out_ref, scratch)

    @pl.when(step == 0)
    def _():
        out_ref[:, 0:2, :] += below_ref[...]

    @pl.when(step == 1)
    def _():
        out_ref[:, 62:64, :] += above_ref[...]


def from_behind(block, axis, distance):
    devices = range(lax.axis_size(axis))
    route = [((i - distance) % len(devices), i) for i in devices]
    return lax.ppermute(block, axis, route)


def on_device(charges, weight_tiles, block_shape, block_box, live_blocks):
    nblk, atoms = charges.shape
    shapes_n, _, cells = weight_tiles.shape
    wflat = weight_tiles.reshape(shapes_n * atoms, cells)
    rows = (nblk // 128, 128)
    vmem = pl.BlockSpec(memory_space=pltpu.VMEM)
    smem = pl.BlockSpec(memory_space=pltpu.SMEM)
    hbm = pl.BlockSpec(memory_space=pl.ANY)
    sent = pl.pallas_call(
        spread_kernel,
        out_shape=jax.ShapeDtypeStruct((KZ, SENT, 128), WIRE),
        in_specs=[smem] + [vmem] * 3 + [hbm] * 2,
        out_specs=hbm,
        scratch_shapes=[
            pltpu.VMEM((GROWS + SPARE, 128), jnp.float32),
            pltpu.VMEM((shapes_n * atoms, cells), jnp.bfloat16),
            pltpu.VMEM((1024, 256), jnp.bfloat16),
            pltpu.VMEM((GROUP, shapes_n * atoms), jnp.bfloat16),
            pltpu.VMEM((GROUP, 1024), jnp.bfloat16),
            pltpu.VMEM((GROUP, 1024), jnp.bfloat16),
            pltpu.VMEM((GROUP, 128), jnp.float32),
            pltpu.VMEM((GROUP, 128), jnp.float32),
            pltpu.VMEM((GROUP * 4, 128), jnp.float32),
            pltpu.VMEM((GROUP * 4, 128), jnp.float32),
            pltpu.VMEM((2, SENT, 128), jnp.float32),
            pltpu.VMEM(rows, jnp.int32),
            pltpu.VMEM(rows, jnp.int32),
            pltpu.VMEM(rows, jnp.int32),
            pltpu.VMEM(rows, jnp.int32),
            pltpu.VMEM(rows, jnp.float32),
            pltpu.SMEM(rows, jnp.int32),
            pltpu.SMEM(rows, jnp.int32),
            pltpu.SMEM(rows, jnp.int32),
            pltpu.SMEM(rows, jnp.int32),
            pltpu.VMEM((KZ, SENT, 128), WIRE),
            pltpu.SemaphoreType.DMA((6,)),
            pltpu.SemaphoreType.DMA((KZ,)),
        ],
        compiler_params=pltpu.CompilerParams(vmem_limit_bytes=56 * 1024 * 1024),
        name="spread",
    )(
        live_blocks,
        charges,
        block_shape.reshape(rows),
        block_box.reshape(rows),
        wflat,
        jnp.asarray(restriction(), jnp.bfloat16),
    )
    got = lax.all_to_all(sent, "bx", split_axis=0, concat_axis=0, tiled=True)
    small = pl.BlockSpec((8, 2, 512), lambda p: (0, 0, 0))
    full = jax.ShapeDtypeStruct((8, 256, 512), jnp.float32)
    scratch = [
        pltpu.VMEM((16 * 80, 128), jnp.float32),
        pltpu.VMEM((128, 128), jnp.float32),
        pltpu.VMEM((4, 512, 128), jnp.float32),
    ]
    params = pltpu.CompilerParams(vmem_limit_bytes=40 * 1024 * 1024)
    down, up = pl.pallas_call(
        edge_kernel,
        out_shape=(jax.ShapeDtypeStruct((8, 2, 512), jnp.float32),) * 2,
        grid=(1,),
        in_specs=[vmem],
        out_specs=(small, small),
        scratch_shapes=scratch,
        compiler_params=params,
        name="edge",
    )(got)
    below = from_behind(up, "by", 1)
    above = from_behind(down, "by", -1)
    inner = pl.pallas_call(
        inner_kernel,
        out_shape=full,
        grid=(2,),
        in_specs=[vmem],
        out_specs=pl.BlockSpec((8, 64, 512), lambda p: (0, p + 1, 0)),
        scratch_shapes=scratch,
        compiler_params=params,
        name="inner",
    )(got)
    return pl.pallas_call(
        outer_kernel,
        out_shape=full,
        grid=(2,),
        in_specs=[vmem, small, small, hbm],
        out_specs=pl.BlockSpec((8, 64, 512), lambda p: (0, 3 * p, 0)),
        scratch_shapes=scratch,
        input_output_aliases={3: 0},
        compiler_params=params,
        name="outer",
    )(got, below, above, inner)


def solution(mesh):
    return jax.shard_map(
        on_device,
        mesh=mesh,
        in_specs=(P(("bx", "by"), None), P(), P(("bx", "by")), P(("bx", "by")), P(("bx", "by"))),
        out_specs=P("bx", "by", None),
        check_vma=False,
    )
```
